32 devices in a mesh: blk: 16 (over z, y, x), head: 2 (over core).
Axes of the slice: x: 2, y: 2, z: 4, core: 2. Of those that a mesh axis runs over, the one named last changes fastest.
Arguments:
- tokens: bfloat16 [512, 1024], P('blk'), may hold values from -6 to 6
- norm_gain: float32 [1024], replicated, may hold values from 0.25 to 1.75
- w_query: bfloat16 [1024, 1024], P(None, 'head')
- w_key: bfloat16 [1024, 1024], P(None, 'head'), may hold values from -0.1875 to 0.1875
- w_value: bfloat16 [1024, 1024], P(None, 'head'), may hold values from -0.1875 to 0.1875
- w_out: bfloat16 [1024, 1024], P('head'), may hold values from -0.1875 to 0.1875
- ffn_gain: float32 [1024], replicated, may hold values from 0.25 to 1.75
- w_gate: bfloat16 [1024, 4096], P(None, 'head'), may hold values from -0.1875 to 0.1875
- w_up: bfloat16 [1024, 4096], P(None, 'head'), may hold values from -0.1875 to 0.1875
- w_down: bfloat16 [4096, 1024], P('head'), may hold values from -0.09375 to 0.09375
- keys: bfloat16 [16384, 1024], P('blk', 'head'), may hold values from -6 to 6
- values: bfloat16 [16384, 1024], P('blk', 'head'), may hold values from -6 to 6
- key_variate: int32 [16384], P('blk'), may hold values from 0 to 3
- query_variate: int32 [512], replicated, may hold values from 0 to 3
- bias: float32 [2, 16], P(None, 'head'), may hold values from -2 to 2
- lengths: int32 [512], replicated, may hold values from 17 to 4096, as said below
- order: int32 [512], replicated, may hold values from 0 to 511, as said below
- live_blocks: int32 [256], P('blk'), may hold values from 0 to 1
Outputs:
- layer_out: bfloat16 [512, 1024], P('blk', 'head')
The draws below stay inside these ranges and needn't reach their ends.
Inputs may be any that keep to these rules, and one draw needn't show every extreme that they name: lengths sum to 16384; the smallest is exactly 17 and the largest exactly 4096. Each request appears once; order[j] // 32 depends only on j % 16.
All inputs are finite; a program needn't handle non-finite values.
Results may differ from the reference program's by a relative error of at most 0.025.
Values may be sent and summed in bfloat16 or wider, within the bound.
No kernel may reach another device: no remote copies, remote signals or barrier semaphores. Data moves between devices by JAX's collectives and lax.ppermute only.
A program may use at most 64 MiB of HBM per device.

```python
import math
import jax
import jax.numpy as jnp
from jax import lax

D = 1024
H = 16
DH = 64
FF = 4096
VARIATES = 4
REQ_DEV = 32
BLOCK = 64
HD = 1024
R = 512
POOL = 16384
NBLK = 256
MAXLEN = 4096
MINLEN = 17


def cache_lengths(key):
    base_key = jax.random.fold_in(key, 101)
    shortest = MINLEN
    leftover = POOL - R * shortest - (MAXLEN - shortest)
    cut_points = jnp.sort(jax.random.randint(jax.random.fold_in(base_key, 1), (R - 3,), 0, leftover + 1, dtype=jnp.int32))
    boundary = jnp.concatenate([jnp.zeros((1,), jnp.int32), cut_points.astype(jnp.int32), jnp.full((1,), leftover, jnp.int32)])
    extras = boundary[1:] - boundary[:-1]
    listed = jnp.concatenate([jnp.full((1,), MAXLEN, jnp.int32), jnp.full((1,), shortest, jnp.int32), shortest + extras])
    shuffle = jax.random.permutation(jax.random.fold_in(base_key, 2), R)
    return listed[shuffle].astype(jnp.int32)


def pool_order(key):
    base_key = jax.random.fold_in(key, 202)
    groups = R // REQ_DEV
    home_list = jax.random.permutation(jax.random.fold_in(base_key, 1), groups).astype(jnp.int32)

    def pick_slots(subkey):
        return jax.random.permutation(subkey, REQ_DEV).astype(jnp.int32)
    within = jax.vmap(pick_slots)(jax.random.split(jax.random.fold_in(base_key, 2), groups))
    position = jnp.arange(R, dtype=jnp.int32)
    home_rows = home_list[position % groups]
    return (home_rows * REQ_DEV + within[home_rows, position // groups]).astype(jnp.int32)


def chosen_requests(key):
    return jax.random.permutation(jax.random.fold_in(key, 303), R)[:4].astype(jnp.int32)


def sign_pattern(key, salt, count):
    return (2 * jax.random.randint(jax.random.fold_in(key, salt), (count,), 0, 2, dtype=jnp.int32) - 1).astype(jnp.float32)


def drawn_rows(key):
    lengths_drawn = cache_lengths(key)
    order_drawn = pool_order(key)
    ends = jnp.cumsum(lengths_drawn[order_drawn]).astype(jnp.int32)
    position = jnp.arange(POOL, dtype=jnp.int32)
    rank = jnp.searchsorted(ends, position, side='right').astype(jnp.int32)
    owner = order_drawn[rank]
    offset = position - (ends[rank] - lengths_drawn[owner])
    match = owner[:, None] == chosen_requests(key)[None, :]
    planted = jnp.any(match, axis=1) & (offset < 8)
    return (match, planted, offset)


def draw_lengths(key, part):
    return cache_lengths(key)


def draw_order(key, part):
    return pool_order(key)


def draw_live_blocks(key, part):
    match, planted, offset = drawn_rows(key)
    coins = jax.random.randint(jax.random.fold_in(key, 808), (NBLK,), 0, 4, dtype=jnp.int32)
    base_live = (coins > 0).astype(jnp.int32)
    position = jnp.arange(POOL, dtype=jnp.int32)
    forced = jnp.zeros((NBLK,), jnp.int32).at[position // BLOCK].max(planted.astype(jnp.int32))
    return jnp.maximum(base_live, forced).astype(jnp.int32)


def draw_tokens(key, part):
    pattern = sign_pattern(key, 606, D)
    column = jnp.arange(D, dtype=jnp.float32) / jnp.float32(D - 1)
    base = jnp.clip(jax.random.normal(jax.random.fold_in(key, 909), (R, D), jnp.float32), -6.0, 6.0)
    ramp = 0.2 + 0.8 * column
    request_ids = jnp.arange(R, dtype=jnp.int32)
    picked = jnp.any(request_ids[:, None] == chosen_requests(key)[None, :], axis=1)
    return jnp.where(picked[:, None], 6.0 * pattern[None, :], base * ramp[None, :]).astype(jnp.bfloat16)


def draw_w_query(key, part):
    token_pattern = sign_pattern(key, 606, D)
    key_pattern = sign_pattern(key, 404, HD)
    base = jnp.clip(jax.random.normal(jax.random.fold_in(key, 707), (D, HD), jnp.float32), -6.0, 6.0) / math.sqrt(D)
    return (base + 6.0 / D * token_pattern[:, None] * key_pattern[None, :]).astype(jnp.bfloat16)


def draw_keys(key, part):
    match, planted, offset = drawn_rows(key)
    pattern = sign_pattern(key, 404, HD)
    noise = jnp.clip(jax.random.normal(jax.random.fold_in(key, 505), (POOL, HD), jnp.float32), -6.0, 6.0)
    strengths = jnp.array([4.5, 3.5, 2.5, 1.5], jnp.float32)
    strength = jnp.sum(jnp.where(match, strengths[None, :], jnp.float32(0.0)), axis=1)
    level = strength - offset.astype(jnp.float32) * (2.0 / (6.0 * math.sqrt(DH)))
    return jnp.where(planted[:, None], level[:, None] * pattern[None, :], noise).astype(jnp.bfloat16)


def place_ends(values, own_key, low, largest):
    place = [jax.random.randint(jax.random.fold_in(own_key, axis), (), 0, length) for axis, length in enumerate(values.shape)]
    main_axis = values.shape.index(max(values.shape))
    beside = place[:main_axis] + [(place[main_axis] + 1) % values.shape[main_axis]] + place[main_axis + 1:]
    return values.at[tuple(place)].set(low).at[tuple(beside)].set(largest)


def steps_of(rng, shape, cuts, low, largest):
    factor_of = 1.0
    for axis_at, blocks in cuts:
        heights = jax.random.uniform(jax.random.fold_in(jax.random.fold_in(rng, 6), axis_at), (blocks,), jnp.float32, low / len(cuts), largest / len(cuts))
        factor_of = factor_of * jnp.repeat(jnp.exp(heights), shape[axis_at] // blocks).reshape((-1,) + (1,) * (len(shape) - 1 - axis_at))
    return factor_of


def normal_values(key, extent, spread, most, shards=(), held_as=jnp.bfloat16):
    level = steps_of(key, extent, shards, -0.22, 0.18) if shards else 1.0
    result = jax.random.normal(key, extent, jnp.float32) * spread * level
    return jnp.minimum(jnp.maximum(result, -most), most).astype(held_as)


def setup_inputs(seed: int = 0) -> dict:
    key_list = jax.random.split(jax.random.key(seed), 19)
    return {
        "tokens": draw_tokens(jax.random.fold_in(key_list[18], 71), 0),
        "norm_gain": jnp.clip(1.0 + 0.15 * jax.random.normal(key_list[1], (D,), jnp.float32), 0.25, 1.75),
        "w_query": draw_w_query(jax.random.fold_in(key_list[18], 71), 0),
        "w_key": normal_values(key_list[3], (D, HD), D ** -0.5, 0.1875, ((1, 2),)),
        "w_value": normal_values(key_list[4], (D, HD), D ** -0.5, 0.1875, ((1, 2),)),
        "w_out": normal_values(key_list[5], (HD, D), HD ** -0.5, 0.1875, ((0, 2),)),
        "ffn_gain": jnp.clip(1.0 + 0.15 * jax.random.normal(key_list[6], (D,), jnp.float32), 0.25, 1.75),
        "w_gate": normal_values(key_list[7], (D, FF), D ** -0.5, 0.1875, ((1, 2),)),
        "w_up": normal_values(key_list[8], (D, FF), D ** -0.5, 0.1875, ((1, 2),)),
        "w_down": normal_values(key_list[9], (FF, D), FF ** -0.5, 0.09375, ((0, 2),)),
        "keys": draw_keys(jax.random.fold_in(key_list[18], 71), 0),
        "values": normal_values(key_list[11], (POOL, HD), 1.0, 6.0, ((0, 16), (1, 2))),
        "key_variate": place_ends(jax.random.randint(key_list[12], (POOL,), 0, VARIATES), jax.random.fold_in(key_list[12], 1), 0, VARIATES - 1).astype(jnp.int32),
        "query_variate": place_ends(jax.random.randint(key_list[13], (R,), 0, VARIATES), jax.random.fold_in(key_list[13], 1), 0, VARIATES - 1).astype(jnp.int32),
        "bias": jnp.clip(jax.random.uniform(key_list[14], (2, H), jnp.float32, -2.0, 2.0) * steps_of(key_list[14], (2, H), ((1, 2),), -0.4, 0.0), -2.0, 2.0),
        "lengths": draw_lengths(jax.random.fold_in(key_list[18], 71), 0),
        "order": draw_order(jax.random.fold_in(key_list[18], 71), 0),
        "live_blocks": draw_live_blocks(jax.random.fold_in(key_list[18], 71), 0),
    }


def normalize(inputs, gain):
    mean_square = lax.optimization_barrier(jnp.mean(inputs * inputs, axis=-1, keepdims=True))
    return inputs * lax.rsqrt(mean_square + 1e-05) * gain

def reference(tokens, norm_gain, w_query, w_key, w_value, w_out, ffn_gain, w_gate, w_up, w_down, keys, values, key_variate, query_variate, bias, lengths, order, live_blocks):
    inputs = tokens.astype(jnp.float32)
    normed = normalize(inputs, norm_gain).astype(jnp.bfloat16)
    query = jnp.dot(normed, w_query, preferred_element_type=jnp.float32).astype(jnp.bfloat16)
    key_new = jnp.dot(normed, w_key, preferred_element_type=jnp.float32).astype(jnp.bfloat16)
    value_new = jnp.dot(normed, w_value, preferred_element_type=jnp.float32).astype(jnp.bfloat16)
    ends = jnp.cumsum(lengths[order]).astype(jnp.int32)
    position = jnp.arange(POOL, dtype=jnp.int32)
    rank = jnp.searchsorted(ends, position, side='right').astype(jnp.int32)
    owner = order[rank]
    live = jnp.repeat(live_blocks, POOL // live_blocks.shape[0]) > 0
    query_heads = query.astype(jnp.float32).reshape(R, H, DH)
    key_heads = keys.astype(jnp.float32).reshape(POOL, H, DH)
    raw = lax.optimization_barrier(jnp.sum(query_heads[owner] * key_heads, axis=2)) / jnp.sqrt(jnp.float32(DH))
    same = key_variate == query_variate[owner]
    score = raw + jnp.where(same[:, None], bias[0][None, :], bias[1][None, :])
    own = lax.optimization_barrier(jnp.sum(query_heads * key_new.astype(jnp.float32).reshape(R, H, DH), axis=2)) / jnp.sqrt(jnp.float32(DH)) + bias[0][None, :]
    masked = jnp.where(live[:, None], score, jnp.float32(-1e+30))
    top = jnp.full((R, H), -1e+30, jnp.float32).at[owner].max(masked)
    top = jnp.maximum(top, own)
    weight = jnp.where(live[:, None], jnp.exp(masked - top[owner]), jnp.float32(0.0))
    own_weight = jnp.exp(own - top)
    total = jax.ops.segment_sum(weight, owner, num_segments=R) + own_weight
    value_heads = values.astype(jnp.float32).reshape(POOL, H, DH)
    summed = jax.ops.segment_sum(weight[:, :, None] * value_heads, owner, num_segments=R)
    summed = summed + own_weight[:, :, None] * value_new.astype(jnp.float32).reshape(R, H, DH)
    attended = (summed / total[:, :, None]).reshape(R, H * DH).astype(jnp.bfloat16)
    mixed = (inputs + jnp.dot(attended, w_out, preferred_element_type=jnp.float32)).astype(jnp.bfloat16)
    hidden_in = normalize(mixed.astype(jnp.float32), ffn_gain).astype(jnp.bfloat16)
    gate = jnp.dot(hidden_in, w_gate, preferred_element_type=jnp.float32)
    upper = jnp.dot(hidden_in, w_up, preferred_element_type=jnp.float32)
    hidden = (jax.nn.silu(gate) * upper).astype(jnp.bfloat16)
    return (mixed.astype(jnp.float32) + jnp.dot(hidden, w_down, preferred_element_type=jnp.float32)).astype(jnp.bfloat16)
```

```python
import functools

import jax
import jax.numpy as jnp
from jax import lax
from jax.experimental import pallas as pl
from jax.experimental.pallas import tpu as pltpu
from jax.sharding import PartitionSpec as P

LANES = 128
SHORTEST = 17
FLOOR = -1e30
F32 = jnp.float32
BF16 = jnp.bfloat16
I32 = jnp.int32


def cdiv(a, b):
    return -(-a // b)


def split_by(x, n):
    if n & (n - 1) == 0:
        return lax.shift_right_logical(x, n.bit_length() - 1), x & (n - 1)
    q = lax.div(x, n)
    return q, x - q * n


def iota(shape, dim):
    return lax.broadcasted_iota(I32, shape, dim)


def dot(a, b):
    return jnp.dot(a, b, preferred_element_type=F32)


def dot_exact(a, b):
    return jnp.dot(a, b, preferred_element_type=F32, precision=lax.Precision.HIGHEST)


def one_hot(mask):
    return jnp.where(mask, F32(1), F32(0)).astype(BF16)


def normalize(inputs, gain):
    mean_square = jnp.mean(inputs * inputs, axis=-1, keepdims=True)
    return inputs * lax.rsqrt(mean_square + 1e-05) * gain


class Sizes:
    def __init__(self, groups, req_dev, pool_dev, block, heads, head_dim):
        self.groups, self.req, self.pool = groups, req_dev, pool_dev
        self.block, self.heads, self.dim = block, heads, head_dim
        self.total = groups * req_dev
        most = (pool_dev - 2) // SHORTEST + 2
        self.slot = cdiv(most, groups)
        self.slots = groups * self.slot
        self.width = heads * head_dim
        self.chunks = self.width // LANES
        self.pair = LANES // head_dim
        self.ask_rows = cdiv(self.chunks * self.slot, 16) * 16
        self.back_rows = cdiv((self.chunks + 1) * self.slot, 16) * 16


def message_rows(z, rows, parts, transpose=False):
    shape = (z.groups * rows, parts * z.slots)
    m_dim, s_dim = (1, 0) if transpose else (0, 1)
    if transpose:
        shape = shape[::-1]
    group, inner = split_by(iota(shape, m_dim), rows)
    part, slot = split_by(inner, z.slot)
    source = part * z.slots + group * z.slot + slot
    return one_hot((source == iota(shape, s_dim)) & (part < parts))


def place_rows(lengths, order, variate, step=512):
    total = order.shape[1]
    step = min(step, total)
    sub = iota((16, total), 0)
    table = jnp.where(
        sub == 0,
        lax.shift_right_logical(lengths, 6),
        jnp.where(sub == 1, lengths & 63, jnp.where(sub == 2, variate, 0)),
    )
    table = table.astype(F32).astype(BF16)
    request = iota((total, step), 0)
    found, sums = [], []
    for at in range(0, total, step):
        found.append(dot(table, one_hot(request == order[:, at : at + step])))
    ordered = jnp.concatenate(found, axis=1) if len(found) > 1 else found[0]
    ordered_low = ordered.astype(BF16)
    for at in range(0, total, step):
        before = one_hot(iota((at + step, step), 0) <= iota((at + step, step), 1) + at)
        sums.append(dot(ordered_low[:, : at + step], before))
    summed = jnp.concatenate(sums, axis=1) if len(sums) > 1 else sums[0]
    ends = summed[0:1] * 64.0 + summed[1:2]
    starts = ends - (ordered[0:1] * 64.0 + ordered[1:2])
    return starts, ends, ordered[2:3]


def ask_kernel(z, tokens_ref, gain_ref, w_query_ref, lengths_ref, order_ref, variate_ref, live_ref,
               ask_ref, query_ref, home_ref, slot_ref, live_out_ref, w_query, sem):
    me = lax.axis_index("blk")
    copy = pltpu.make_async_copy(w_query_ref, w_query, sem)
    copy.start()
    order = order_ref[...]
    starts, ends, variates = place_rows(lengths_ref[...], order, variate_ref[...])
    shape = (z.slots, z.total)
    place = iota(shape, 1)
    other, turn = split_by(iota((z.slots, 1), 0), z.slot)
    home_of, local = split_by(order, z.req)

    def choose(home, pool):
        low = (pool * z.pool).astype(F32)
        first = jnp.sum(jnp.where(ends <= low, F32(1), F32(0)), axis=1, keepdims=True)
        first = first.astype(I32) + turn * z.groups
        return (
            (home_of == home)
            & (starts < low + F32(z.pool))
            & (place >= first)
            & (place < first + z.groups)
        )

    mine = choose(me, other)
    row = jnp.sum(jnp.where(mine, local.astype(F32) + 1.0, F32(0)), axis=1, keepdims=True) - 1.0
    row = row.astype(I32)
    home_ref[...] = jnp.broadcast_to(row, home_ref.shape)
    theirs = choose(other, jnp.full((1, 1), me, I32))
    low = (me * z.pool).astype(F32)
    begin = jnp.sum(jnp.where(theirs, starts - low, F32(0)), axis=1, keepdims=True)
    finish = jnp.sum(jnp.where(theirs, ends - low, F32(0)), axis=1, keepdims=True)
    kind = jnp.sum(jnp.where(theirs, variates, F32(0)), axis=1, keepdims=True)
    lane = iota((z.slots, LANES), 1)
    slot_ref[...] = jnp.where(
        lane == 0, begin, jnp.where(lane == 1, finish, kind)
    ).astype(I32)
    blocks = live_ref.shape[1]
    spread = one_hot(
        split_by(iota((blocks, z.pool), 1), z.block)[0] == iota((blocks, z.pool), 0)
    )
    live = jnp.broadcast_to(live_ref[...].astype(F32).astype(BF16), (16, blocks))
    live_out_ref[...] = dot(live, spread)[:8].astype(I32)

    normed = normalize(tokens_ref[...].astype(F32), gain_ref[...]).astype(BF16)
    copy.wait()
    query = dot(normed, w_query[...]).astype(BF16)
    query_ref[...] = query
    picked = dot(one_hot(row == iota((z.slots, z.req), 1)), query).astype(BF16)
    stacked = jnp.concatenate(
        [picked[:, c * LANES : (c + 1) * LANES] for c in range(z.chunks)], axis=0
    )
    ask_ref[...] = dot(message_rows(z, z.ask_rows, z.chunks), stacked).astype(BF16)


def pieces(z, columns):
    rows = columns[0].shape[0]
    lane = iota((rows, LANES), 1)
    full = jnp.zeros((rows, LANES), F32)
    for h, column in enumerate(columns):
        full = jnp.where((lane & (z.heads - 1)) == h, column, full)
    high = full.astype(BF16).astype(F32)
    rest = full - high
    middle = rest.astype(BF16).astype(F32)
    last = rest - middle
    n = z.heads
    return jnp.where(
        lane < n, high, jnp.where(lane < 2 * n, middle, jnp.where(lane < 3 * n, last, F32(0)))
    ).astype(BF16)


def own_kernel(z, tokens_ref, gain_ref, w_key_ref, w_value_ref, query_ref, bias_ref,
               value_ref, stat_ref):
    normed = normalize(tokens_ref[...].astype(F32), gain_ref[...]).astype(BF16)
    key_new = dot(normed, w_key_ref[...]).astype(BF16)
    value_ref[...] = dot(normed, w_value_ref[...]).astype(BF16)
    product = query_ref[...].astype(F32) * key_new.astype(F32)
    columns = []
    for h in range(z.heads):
        c, inner = divmod(h, z.pair)
        part = product[:, c * LANES : (c + 1) * LANES]
        lane_head = split_by(iota(part.shape, 1), z.dim)[0]
        raw = jnp.sum(jnp.where(lane_head == inner, part, F32(0)), axis=1, keepdims=True)
        columns.append(raw * F32(z.dim**-0.5) + bias_ref[0, h])
    stat_ref[...] = pieces(z, columns)


def attend_kernel(z, ask_ref, keys_ref, values_ref, slot_ref, variate_ref, live_ref, bias_ref, back_ref):
    stacked = dot(message_rows(z, z.ask_rows, z.chunks, transpose=True), ask_ref[...])
    begin, finish, kind = slot_ref[:, 0:1], slot_ref[:, 1:2], slot_ref[:, 2:3]
    shape = (z.slots, z.pool)
    token = iota(shape, 1)
    used = (token >= begin) & (token < finish) & (live_ref[0:1] > 0)
    same = variate_ref[...] == kind
    lane = split_by(iota((z.slots, LANES), 1), z.dim)[0]
    columns, parts = [], []
    for c in range(z.chunks):
        asked = stacked[c * z.slots : (c + 1) * z.slots] * F32(z.dim**-0.5)
        wide = jnp.concatenate(
            [jnp.where(lane == i, asked, F32(0)) for i in range(z.pair)], axis=0
        ).astype(BF16)
        chunk = slice(c * LANES, (c + 1) * LANES)
        score = lax.dot_general(
            wide, keys_ref[:, chunk], (((1,), (1,)), ((), ())), preferred_element_type=F32
        )
        weights, scale = [], []
        for i in range(z.pair):
            h = c * z.pair + i
            one = score[i * z.slots : (i + 1) * z.slots]
            one = one + jnp.where(same, bias_ref[0, h], bias_ref[1, h])
            one = jnp.where(used, one, F32(FLOOR))
            top = jnp.maximum(jnp.max(one, axis=1, keepdims=True), F32(FLOOR * 0.1))
            weight = jnp.exp(one - top).astype(BF16)
            total = jnp.sum(weight.astype(F32), axis=1, keepdims=True)
            some = total > 0
            safe = jnp.where(some, total, F32(1))
            columns.append(jnp.where(some, top + jnp.log(safe), F32(FLOOR)))
            scale.append(1.0 / safe)
            weights.append(weight)
        summed = dot(jnp.concatenate(weights, axis=0), values_ref[:, chunk])
        summed = summed * jnp.concatenate(scale, axis=0)
        part = summed[: z.slots]
        for i in range(1, z.pair):
            part = jnp.where(lane == i, summed[i * z.slots : (i + 1) * z.slots], part)
        parts.append(part.astype(BF16))
    parts.append(pieces(z, columns))
    back_ref[...] = dot(
        message_rows(z, z.back_rows, z.chunks + 1), jnp.concatenate(parts, axis=0)
    ).astype(BF16)


def merge_kernel(z, back_ref, home_ref, value_ref, stat_ref, w_out_ref, part_ref):
    stacked = dot(message_rows(z, z.back_rows, z.chunks + 1, transpose=True), back_ref[...]).astype(BF16)
    stat = jnp.concatenate([stacked[z.chunks * z.slots :], stat_ref[...]], axis=0)
    rows = z.slots + z.req
    wide = z.heads * z.req
    head_at, _ = split_by(iota((LANES, wide), 1), z.req)
    from_lane = iota((LANES, wide), 0)
    spread = one_hot(((from_lane & (z.heads - 1)) == head_at) & (from_lane < 3 * z.heads))
    level = dot(stat, spread)
    _, request = split_by(iota((rows, wide), 1), z.req)
    owner = jnp.concatenate([home_ref[:, 0:1], iota((z.req, 1), 0)], axis=0)
    match = owner == request
    level = jnp.where(match, level, F32(FLOOR))
    top = jnp.max(level, axis=0, keepdims=True)
    weight = jnp.where(match, jnp.exp(level - top), F32(0))
    weight = weight / jnp.sum(weight, axis=0, keepdims=True)
    high = weight.astype(BF16)
    low = (weight - high.astype(F32)).astype(BF16)
    lane = split_by(iota((z.req, LANES), 1), z.dim)[0]
    attended = []
    for c in range(z.chunks):
        held = jnp.concatenate(
            [stacked[c * z.slots : (c + 1) * z.slots], value_ref[:, c * LANES : (c + 1) * LANES]],
            axis=0,
        )
        dims = (((0,), (0,)), ((), ()))
        summed = lax.dot_general(high, held, dims, preferred_element_type=F32)
        summed = summed + lax.dot_general(low, held, dims, preferred_element_type=F32)
        base = c * z.pair * z.req
        part = summed[base : base + z.req]
        for i in range(1, z.pair):
            part = jnp.where(lane == i, summed[base + i * z.req : base + (i + 1) * z.req], part)
        attended.append(part.astype(BF16))
    part_ref[...] = dot(jnp.concatenate(attended, axis=1), w_out_ref[...]).astype(BF16)


def call(kernel, out, operands, specs, scratch=(), flops=0, nbytes=0, name=None):
    return pl.pallas_call(
        kernel,
        out_shape=[jax.ShapeDtypeStruct(s, d) for s, d in out],
        in_specs=specs,
        out_specs=[pl.BlockSpec(memory_space=pltpu.VMEM)] * len(out),
        scratch_shapes=list(scratch),
        compiler_params=pltpu.CompilerParams(vmem_limit_bytes=24 * 1024 * 1024),
        cost_estimate=pl.CostEstimate(flops=flops, bytes_accessed=nbytes, transcendentals=0),
        name=name,
    )(*operands)


def head_sum(x):
    if lax.axis_size("head") == 2:
        return x.astype(F32) + lax.ppermute(x, "head", [(0, 1), (1, 0)]).astype(F32)
    return lax.psum(x.astype(F32), "head")


def body(
    tokens,
    norm_gain,
    w_query,
    w_key,
    w_value,
    w_out,
    ffn_gain,
    w_gate,
    w_up,
    w_down,
    keys,
    values,
    key_variate,
    query_variate,
    bias,
    lengths,
    order,
    live_blocks,
):
    groups = lax.axis_size("blk")
    z = Sizes(
        groups,
        tokens.shape[0],
        keys.shape[0],
        keys.shape[0] // live_blocks.shape[0],
        bias.shape[1],
        w_query.shape[1] // bias.shape[1],
    )
    d_model = tokens.shape[1]
    head_count = lax.axis_size("head")
    width_local = d_model // head_count
    vmem = pl.BlockSpec(memory_space=pltpu.VMEM)
    smem = pl.BlockSpec(memory_space=pltpu.SMEM)
    anywhere = pl.BlockSpec(memory_space=pl.ANY)
    gain = norm_gain.reshape(1, -1)
    ask, query, home, slot, live = call(
        functools.partial(ask_kernel, z),
        [
            ((groups * z.ask_rows, LANES), BF16),
            ((z.req, z.width), BF16),
            ((z.slots, LANES), I32),
            ((z.slots, LANES), I32),
            ((8, z.pool), I32),
        ],
        (tokens, gain, w_query, lengths.reshape(1, -1), order.reshape(1, -1),
         query_variate.reshape(1, -1), live_blocks.reshape(1, -1)),
        [vmem, vmem, anywhere, vmem, vmem, vmem, vmem],
        scratch=[pltpu.VMEM(w_query.shape, BF16), pltpu.SemaphoreType.DMA],
        flops=10**9, nbytes=2 * 10**6, name="ask",
    )
    asked = lax.all_to_all(ask.reshape(groups, z.ask_rows, LANES), "blk", 0, 0).reshape(ask.shape)
    value_new, own = call(
        functools.partial(own_kernel, z),
        [((z.req, z.width), BF16), ((z.req, LANES), BF16)],
        (tokens, gain, w_key, w_value, query, bias),
        [vmem, vmem, vmem, vmem, vmem, smem],
        flops=10**9, nbytes=3 * 10**6, name="own",
    )
    (back,) = call(
        functools.partial(attend_kernel, z),
        [((groups * z.back_rows, LANES), BF16)],
        (asked, keys, values, slot, key_variate.reshape(1, -1), live, bias),
        [vmem, vmem, vmem, vmem, vmem, vmem, smem],
        flops=10**9, nbytes=3 * 10**6, name="attend",
    )
    returned = lax.all_to_all(back.reshape(groups, z.back_rows, LANES), "blk", 0, 0).reshape(back.shape)
    (part,) = call(
        functools.partial(merge_kernel, z),
        [((z.req, d_model), BF16)],
        (returned, home, value_new, own, w_out),
        [vmem] * 5,
        flops=10**9, nbytes=2 * 10**6, name="merge",
    )
    mixed = (tokens.astype(F32) + head_sum(part)).astype(BF16).astype(F32)
    hidden_in = normalize(mixed, ffn_gain).astype(BF16)
    gate = dot(hidden_in, w_gate)
    upper = dot(hidden_in, w_up)
    hidden = (jax.nn.silu(gate) * upper).astype(BF16)
    down = dot(hidden, w_down).astype(BF16)
    at = lax.axis_index("head")
    mixed_here = lax.dynamic_slice_in_dim(mixed, at * width_local, width_local, 1)
    if head_count == 2:
        here = lax.dynamic_slice_in_dim(down, at * width_local, width_local, 1)
        there = lax.dynamic_slice_in_dim(down, (1 - at) * width_local, width_local, 1)
        summed = here.astype(F32) + lax.ppermute(there, "head", [(0, 1), (1, 0)]).astype(F32)
    else:
        summed = lax.psum_scatter(down, "head", scatter_dimension=1, tiled=True).astype(F32)
    return (mixed_here + summed).astype(BF16)


def solution(mesh):
    placed = (
        P("blk", None),
        P(),
        P(None, "head"),
        P(None, "head"),
        P(None, "head"),
        P("head", None),
        P(),
        P(None, "head"),
        P(None, "head"),
        P("head", None),
        P("blk", "head"),
        P("blk", "head"),
        P("blk"),
        P(),
        P(None, "head"),
        P(),
        P(),
        P("blk"),
    )
    return jax.shard_map(
        body, mesh=mesh, in_specs=placed, out_specs=P("blk", "head"), check_vma=False
    )
```

```python
import functools

import jax
import jax.numpy as jnp
from jax import lax
from jax.experimental import pallas as pl
from jax.experimental.pallas import tpu as pltpu
from jax.sharding import PartitionSpec as P

LANES = 128
SHORTEST = 17
WHOLE = 63
FLOOR = -1e30
AHEAD = 12
F32 = jnp.float32
BF16 = jnp.bfloat16
I32 = jnp.int32


def cdiv(a, b):
    return -(-a // b)


def split_by(x, n):
    if n & (n - 1) == 0:
        return lax.shift_right_logical(x, n.bit_length() - 1), x & (n - 1)
    q = lax.div(x, n)
    return q, x - q * n


def iota(shape, dim):
    return lax.broadcasted_iota(I32, shape, dim)


def dot(a, b):
    return jnp.dot(a, b, preferred_element_type=F32)


def dot_exact(a, b):
    return jnp.dot(a, b, preferred_element_type=F32, precision=lax.Precision.HIGHEST)


def one_hot(mask):
    return jnp.where(mask, F32(1), F32(0)).astype(BF16)


def normalize(inputs, gain):
    mean_square = jnp.mean(inputs * inputs, axis=-1, keepdims=True)
    return inputs * lax.rsqrt(mean_square + 1e-05) * gain


class Sizes:
    def __init__(self, groups, cores, req_dev, pool_dev, block, heads, head_dim):
        self.groups, self.cores, self.req, self.pool = groups, cores, req_dev, pool_dev
        self.block, self.heads, self.dim = block, heads, head_dim
        self.total = groups * req_dev
        most = (pool_dev - 2) // SHORTEST + 2
        self.slot = cdiv(most, groups)
        self.slots = groups * self.slot
        self.width = heads * head_dim
        self.chunks = self.width // LANES
        self.wide = min(self.width, 2 * LANES)
        self.pair = LANES // head_dim
        self.ask_rows = cdiv(self.chunks * self.slot, 16) * 16
        self.back_rows = cdiv((self.chunks + 1) * self.slot, 8) * 8


def message_rows(z, rows, parts, cores=1, core=None, transpose=False):
    many, few = z.groups * cores * rows, parts * z.slots
    at = iota((1, many) if transpose else (many, 1), 1 if transpose else 0)
    device, inner = split_by(at, rows)
    group, its_core = split_by(device, cores)
    part, slot = split_by(inner, z.slot)
    source = part * z.slots + group * z.slot + slot
    used = part < parts
    if core is not None:
        used = used & (its_core == core)
    source = jnp.where(used, source, -1)
    shape = (few, many) if transpose else (many, few)
    return one_hot(source == iota(shape, 0 if transpose else 1))


def place_rows(lengths, order, variate, step=512):
    total = order.shape[1]
    step = min(step, total)
    sub = iota((16, total), 0)
    table = jnp.where(
        sub == 0,
        lax.shift_right_logical(lengths, 6),
        jnp.where(sub == 1, lengths & 63, jnp.where(sub == 2, variate, 0)),
    )
    table = table.astype(F32).astype(BF16)
    request = iota((total, step), 0)
    found, sums = [], []
    for at in range(0, total, step):
        found.append(dot(table, one_hot(request == order[:, at : at + step])))
    ordered = jnp.concatenate(found, axis=1) if len(found) > 1 else found[0]
    ordered_low = ordered.astype(BF16)
    for at in range(0, total, step):
        before = one_hot(iota((at + step, step), 0) <= iota((at + step, step), 1) + at)
        sums.append(dot(ordered_low[:, : at + step], before))
    summed = jnp.concatenate(sums, axis=1) if len(sums) > 1 else sums[0]
    ends = summed[0:1] * 64.0 + summed[1:2]
    starts = ends - (ordered[0:1] * 64.0 + ordered[1:2])
    return starts, ends, ordered[2:3]


def fetch(pairs, sems):
    copies = [pltpu.make_async_copy(src, dst, sems.at[i]) for i, (src, dst) in enumerate(pairs)]
    for copy in copies:
        copy.start()
    return copies


def ask_kernel(z, lengths_hbm, order_hbm, variate_hbm, live_hbm, key_variate_hbm, bias_hbm, tokens_hbm,
               gain_hbm, w_query_hbm, ask_ref, rows_ref, facts_ref, home_ref,
               bias_ref, lengths_ref, order_ref, variate_ref, live_ref, key_variate_ref, tokens_ref,
               gain_ref, w_query_ref, sems):
    me = lax.axis_index("blk")
    copies = fetch(
        [
            (lengths_hbm, lengths_ref),
            (order_hbm, order_ref),
            (variate_hbm, variate_ref),
            (live_hbm, live_ref),
            (key_variate_hbm, key_variate_ref),
            (bias_hbm, bias_ref),
            (tokens_hbm, tokens_ref),
            (gain_hbm, gain_ref),
            (w_query_hbm, w_query_ref),
        ],
        sems,
    )
    for copy in copies[:6]:
        copy.wait()
    order = order_ref[...]
    starts, ends, variates = place_rows(lengths_ref[...], order, variate_ref[...])
    shape = (z.slots, z.total)
    place = iota(shape, 1)
    other, turn = split_by(iota((z.slots, 1), 0), z.slot)
    home_of, local = split_by(order, z.req)

    def choose(home, pool):
        low = (pool * z.pool).astype(F32)
        first = jnp.sum(jnp.where(ends <= low, F32(1), F32(0)), axis=1, keepdims=True)
        first = first.astype(I32) + turn * z.groups
        return (
            (home_of == home)
            & (starts < low + F32(z.pool))
            & (place >= first)
            & (place < first + z.groups)
        )

    mine = choose(me, other)
    row = jnp.sum(jnp.where(mine, local.astype(F32) + 1.0, F32(0)), axis=1, keepdims=True) - 1.0
    row = row.astype(I32)
    theirs = choose(other, jnp.full((1, 1), me, I32))
    low = (me * z.pool).astype(F32)
    begin = jnp.sum(jnp.where(theirs, starts - low, F32(0)), axis=1, keepdims=True)
    finish = jnp.sum(jnp.where(theirs, ends - low, F32(0)), axis=1, keepdims=True)
    kind = jnp.sum(jnp.where(theirs, variates, F32(0)), axis=1, keepdims=True)
    lane = iota((z.slots, LANES), 1)
    facts = jnp.where(lane == 0, begin, jnp.where(lane == 1, finish, kind))
    facts_ref[8:, 0:LANES] = facts
    home_ref[...] = jnp.broadcast_to(row, home_ref.shape)
    blocks = live_ref.shape[1]
    spread = one_hot(
        split_by(iota((blocks, z.pool), 1), z.block)[0] == iota((blocks, z.pool), 0)
    )
    live = jnp.broadcast_to(live_ref[...].astype(F32).astype(BF16), (16, blocks))
    kinds = jnp.where(dot(live, spread)[:1] > 0, key_variate_ref[...], -1)
    facts_ref[0:1, :] = kinds.astype(F32)
    facts_ref[1:3, 0 : z.heads] = bias_ref[...]

    for copy in copies[6:]:
        copy.wait()
    normed = normalize(tokens_ref[...].astype(F32), gain_ref[...]).astype(BF16)
    rows_ref[:, z.width :] = normed
    query = dot(normed, w_query_ref[...]).astype(BF16)
    rows_ref[:, : z.width] = query
    picked = dot(one_hot(row == iota((z.slots, z.req), 1)), query).astype(BF16)
    stacked = jnp.concatenate(
        [picked[:, c * LANES : (c + 1) * LANES] for c in range(z.chunks)], axis=0
    )
    ask_ref[...] = dot(message_rows(z, z.ask_rows, z.chunks), stacked).astype(BF16)


def pieces(z, columns):
    rows = columns[0].shape[0]
    lane = iota((rows, LANES), 1)
    full = jnp.zeros((rows, LANES), F32)
    for h, column in enumerate(columns):
        full = jnp.where((lane & (z.heads - 1)) == h, column, full)
    high = full.astype(BF16).astype(F32)
    rest = full - high
    middle = rest.astype(BF16).astype(F32)
    last = rest - middle
    n = z.heads
    return jnp.where(
        lane < n, high, jnp.where(lane < 2 * n, middle, jnp.where(lane < 3 * n, last, F32(0)))
    ).astype(BF16)


def hold_kernel(*refs):
    refs[-1][...] = jnp.zeros(refs[-1].shape, F32)


def own_kernel(z, after_ref, rows_ref, facts_ref, w_key_ref, w_value_ref, value_ref, stat_ref):
    del after_ref
    normed = rows_ref[:, z.width :]
    key_new = dot(normed, w_key_ref[...]).astype(BF16)
    product = rows_ref[:, : z.width].astype(F32) * key_new.astype(F32)
    columns = []
    for h in range(z.heads):
        c, inner = divmod(h, z.pair)
        part = product[:, c * LANES : (c + 1) * LANES]
        lane_head = split_by(iota(part.shape, 1), z.dim)[0]
        raw = jnp.sum(jnp.where(lane_head == inner, part, F32(0)), axis=1, keepdims=True)
        columns.append(raw * F32(z.dim**-0.5) + facts_ref[1:2, h : h + 1])
    stat_ref[...] = pieces(z, columns)
    value_ref[...] = dot(normed, w_value_ref[...]).astype(BF16)


def feed_kernel(steps, tokens_ref, part_ref, other_ref, gain_ref, w_gate_ref, w_up_ref, w_down_ref,
                mixed_ref, down_ref):
    mixed = tokens_ref[...].astype(F32) + (part_ref[...].astype(F32) + other_ref[...].astype(F32))
    mixed = mixed.astype(BF16).astype(F32)
    hidden_in = normalize(mixed, gain_ref[...]).astype(BF16)
    units = w_gate_ref.shape[1] // steps
    total = jnp.zeros(mixed.shape, F32)
    for step in range(steps):
        at = slice(step * units, (step + 1) * units)
        gate = dot(hidden_in, w_gate_ref[:, at])
        upper = dot(hidden_in, w_up_ref[:, at])
        hidden = (jax.nn.silu(gate) * upper).astype(BF16)
        total = total + dot(hidden, w_down_ref[at, :])
    mixed_ref[...] = mixed.astype(BF16)
    down_ref[...] = total.astype(BF16)


def attend_kernel(z, ask_ref, keys_ref, values_ref, facts_ref, after_ref, back_ref, done_ref):
    del after_ref
    done_ref[...] = jnp.zeros(done_ref.shape, F32)
    stacked = dot(message_rows(z, z.ask_rows, z.chunks, transpose=True), ask_ref[...])
    begin, finish, kind = facts_ref[8:, 0:1], facts_ref[8:, 1:2], facts_ref[8:, 2:3]
    token = iota((z.slots, z.pool), 1).astype(F32)
    kinds = facts_ref[0:1, :]
    used = (token >= begin) & (token < finish) & (kinds >= 0)
    same = kinds == kind
    lane = split_by(iota((z.slots, z.wide), 1), z.dim)[0]
    many = z.wide // z.dim
    each = z.wide // LANES
    columns, parts = [], []
    for c in range(z.width // z.wide):
        asked = jnp.concatenate(
            [stacked[(c * each + i) * z.slots : (c * each + i + 1) * z.slots] for i in range(each)], axis=1
        )
        asked = (asked * F32(z.dim**-0.5)).astype(BF16)
        blocks = jnp.concatenate(
            [jnp.where(lane == i, asked, jnp.zeros_like(asked)) for i in range(many)], axis=0
        )
        chunk = slice(c * z.wide, (c + 1) * z.wide)
        score = lax.dot_general(
            blocks, keys_ref[:, chunk], (((1,), (1,)), ((), ())), preferred_element_type=F32
        )
        weights, scale = [], []
        for i in range(many):
            h = c * many + i
            one = score[i * z.slots : (i + 1) * z.slots]
            one = one + jnp.where(same, facts_ref[1:2, h : h + 1], facts_ref[2:3, h : h + 1])
            one = jnp.where(used, one, F32(FLOOR))
            top = jnp.maximum(jnp.max(one, axis=1, keepdims=True), F32(FLOOR * 0.1))
            weight = jnp.exp(one - top)
            total = jnp.sum(weight, axis=1, keepdims=True)
            some = total > 0
            safe = jnp.where(some, total, F32(1))
            columns.append(jnp.where(some, top + jnp.log(safe), F32(FLOOR)))
            scale.append(1.0 / safe)
            weights.append(weight.astype(BF16))
        summed = dot(jnp.concatenate(weights, axis=0), values_ref[:, chunk])
        part = summed[: z.slots] * scale[0]
        for i in range(1, many):
            part = jnp.where(lane == i, summed[i * z.slots : (i + 1) * z.slots] * scale[i], part)
        part = part.astype(BF16)
        parts += [part[:, i * LANES : (i + 1) * LANES] for i in range(each)]
    parts.append(pieces(z, columns))
    back_ref[...] = dot(
        message_rows(z, z.back_rows, z.chunks + 1, z.cores), jnp.concatenate(parts, axis=0)
    ).astype(BF16)


def merged(z, stacked, owner, value, stat):
    stat = jnp.concatenate([stacked[z.chunks * z.slots :], stat], axis=0)
    rows = z.slots + z.req
    wide = z.heads * z.req
    head_at, _ = split_by(iota((LANES, wide), 1), z.req)
    from_lane = iota((LANES, wide), 0)
    spread = one_hot(((from_lane & (z.heads - 1)) == head_at) & (from_lane < 3 * z.heads))
    level = dot(stat, spread)
    _, request = split_by(iota((rows, wide), 1), z.req)
    match = owner == request
    level = jnp.where(match, level, F32(FLOOR))
    top = jnp.max(level, axis=0, keepdims=True)
    weight = jnp.where(match, jnp.exp(level - top), F32(0))
    weight = weight / jnp.sum(weight, axis=0, keepdims=True)
    high = weight.astype(BF16)
    low = (weight - high.astype(F32)).astype(BF16)
    held = jnp.concatenate(
        [
            jnp.concatenate([stacked[c * z.slots : (c + 1) * z.slots] for c in range(z.chunks)], axis=1),
            value,
        ],
        axis=0,
    )
    dims = (((0,), (0,)), ((), ()))
    summed = lax.dot_general(high, held, dims, preferred_element_type=F32)
    summed = summed + lax.dot_general(low, held, dims, preferred_element_type=F32)
    lane = split_by(iota((z.req, z.width), 1), z.dim)[0]
    attended = summed[: z.req]
    for h in range(1, z.heads):
        attended = jnp.where(lane == h, summed[h * z.req : (h + 1) * z.req], attended)
    return attended.astype(BF16)


def tail_kernel(z, steps, *refs):
    n = z.cores
    count = 4 + 3 * n
    given, gate_hbm, up_hbm, down_hbm = refs[:count], *refs[count : count + 3]
    refs = refs[count + 3 :]
    here_ref, away_refs = refs[0], refs[1:n]
    held, gate_ref, up_ref, down_ref, total_ref, sems = refs[n : n + count], *refs[n + count :]
    units = gate_ref.shape[1] // steps
    pairs = list(zip(given, held))
    for step in range(steps):
        at = slice(step * units, (step + 1) * units)
        pairs += [
            (gate_hbm.at[:, at], gate_ref.at[:, at]),
            (up_hbm.at[:, at], up_ref.at[:, at]),
            (down_hbm.at[at, :], down_ref.at[at, :]),
        ]
    copies = [pltpu.make_async_copy(src, dst, sems.at[i]) for i, (src, dst) in enumerate(pairs)]
    ahead = count + AHEAD
    for copy in copies[:ahead]:
        copy.start()
    for copy in copies[:count]:
        copy.wait()
    back_ref, home_ref, tokens_ref, gain_ref = held[:4]
    stats, values, outs = held[4 : 4 + n], held[4 + n : 4 + 2 * n], held[4 + 2 * n : 4 + 3 * n]
    me = lax.axis_index("head")
    owner = jnp.concatenate([home_ref[:, 0:1], iota((z.req, 1), 0)], axis=0)
    mixed = None
    for i in range(n):
        core = lax.rem(me + i, n)
        choose = message_rows(z, z.back_rows, z.chunks + 1, n, core, transpose=True)
        stacked = dot(choose, back_ref[...]).astype(BF16)
        attended = merged(z, stacked, owner, values[i][...], stats[i][...])
        term = dot(attended, outs[i][...])
        mixed = term if mixed is None else mixed + term
    mixed = (tokens_ref[...].astype(F32) + mixed).astype(BF16).astype(F32)
    hidden_in = normalize(mixed, gain_ref[...]).astype(BF16)
    total = jnp.zeros(mixed.shape, F32)
    for step in range(steps):
        at = slice(step * units, (step + 1) * units)
        for at_copy in range(count + 3 * step, count + 3 * step + 3):
            copies[at_copy].wait()
            if at_copy + AHEAD < len(copies):
                copies[at_copy + AHEAD].start()
        gate = dot(hidden_in, gate_ref[:, at])
        upper = dot(hidden_in, up_ref[:, at])
        hidden = (jax.nn.silu(gate) * upper).astype(BF16)
        total = total + dot(hidden, down_ref[at, :])
    width = mixed.shape[1] // n

    def block(i):
        return pl.ds(pl.multiple_of(lax.rem(me + i, n) * width, width), width)

    total_ref[0] = total
    total_ref[1] = mixed
    here_ref[...] = total_ref[0, :, block(0)] + total_ref[1, :, block(0)]
    for i in range(1, n):
        away_refs[i - 1][...] = total_ref[0, :, block(i)].astype(BF16)


VMEM = pl.BlockSpec(memory_space=pltpu.VMEM)
HBM = pl.BlockSpec(memory_space=pltpu.HBM)


def call(kernel, out, operands, specs, scratch=(), name=None, limit=16):
    return pl.pallas_call(
        kernel,
        out_shape=[jax.ShapeDtypeStruct(s, d) for s, d in out],
        in_specs=specs,
        out_specs=[VMEM] * len(out),
        scratch_shapes=list(scratch),
        compiler_params=pltpu.CompilerParams(vmem_limit_bytes=int(limit * 1024 * 1024)),
        cost_estimate=pl.CostEstimate(flops=10**10, bytes_accessed=10**7, transcendentals=0),
        name=name,
    )(*operands)


def from_core(x, shift):
    n = lax.axis_size("head")
    return lax.ppermute(x, "head", [((i + shift) % n, i) for i in range(n)])


def all_cores(x):
    return [x] + [from_core(x, i) for i in range(1, lax.axis_size("head"))]


def body(
    tokens,
    norm_gain,
    w_query,
    w_key,
    w_value,
    w_out,
    ffn_gain,
    w_gate,
    w_up,
    w_down,
    keys,
    values,
    key_variate,
    query_variate,
    bias,
    lengths,
    order,
    live_blocks,
):
    groups = lax.axis_size("blk")
    head_count = lax.axis_size("head")
    z = Sizes(
        groups,
        head_count,
        tokens.shape[0],
        keys.shape[0],
        keys.shape[0] // live_blocks.shape[0],
        bias.shape[1],
        w_query.shape[1] // bias.shape[1],
    )
    d_model = tokens.shape[1]
    width_local = d_model // head_count
    row = lambda x: x.reshape(1, -1)
    small = (row(lengths), row(order), row(query_variate), row(live_blocks), row(key_variate))
    operands = small + (bias, tokens, row(norm_gain), w_query)
    token = ((8, LANES), F32)
    ask, rows, facts, home = call(
        functools.partial(ask_kernel, z),
        [
            ((groups * z.ask_rows, LANES), BF16),
            ((z.req, z.width + d_model), BF16),
            ((8 + z.slots, z.pool), F32),
            ((z.slots, LANES), I32),
        ],
        operands,
        [HBM] * len(operands),
        scratch=[pltpu.VMEM((2, z.heads), F32)]
        + [pltpu.VMEM(x.shape, x.dtype) for x in small + operands[6:]]
        + [pltpu.SemaphoreType.DMA((len(operands),))],
        name="ask",
        limit=WHOLE,
    )
    asked = lax.all_to_all(ask.reshape(groups, z.ask_rows, LANES), "blk", 0, 0).reshape(ask.shape)
    (held,) = call(hold_kernel, [token], (facts, keys, values), [VMEM] * 3, name="hold")
    back, done = call(
        functools.partial(attend_kernel, z),
        [((groups * head_count * z.back_rows, LANES), BF16), token],
        (asked, keys, values, facts, held),
        [VMEM] * 5,
        name="attend",
    )
    returned = lax.all_to_all(
        back.reshape(groups * head_count, z.back_rows, LANES), ("blk", "head"), 0, 0
    ).reshape(back.shape)
    value_new, own = call(
        functools.partial(own_kernel, z),
        [((z.req, z.width), BF16), ((z.req, LANES), BF16)],
        (done, rows, facts, w_key, w_value),
        [VMEM] * 5,
        name="own",
    )
    w_out_after, _ = lax.optimization_barrier((w_out, held))
    outs = [w_out] + [from_core(w_out_after, i) for i in range(1, head_count)]
    given = (returned, home, tokens, row(ffn_gain), *all_cores(own), *all_cores(value_new), *outs)
    feed = (w_gate, w_up, w_down)
    steps = cdiv(w_gate.shape[1], 512)
    here, *away = call(
        functools.partial(tail_kernel, z, steps),
        [((z.req, width_local), F32)] + [((z.req, width_local), BF16)] * (head_count - 1),
        given + feed,
        [HBM] * (len(given) + 3),
        scratch=[pltpu.VMEM(x.shape, x.dtype) for x in given + feed]
        + [pltpu.VMEM((2, z.req, d_model), F32), pltpu.SemaphoreType.DMA((len(given) + 3 * steps,))],
        name="tail",
        limit=48,
    )
    for i, x in enumerate(away, 1):
        here = here + from_core(x, head_count - i).astype(F32)
    return here.astype(BF16)


def solution(mesh):
    placed = (
        P("blk", None),
        P(),
        P(None, "head"),
        P(None, "head"),
        P(None, "head"),
        P("head", None),
        P(),
        P(None, "head"),
        P(None, "head"),
        P("head", None),
        P("blk", "head"),
        P("blk", "head"),
        P("blk"),
        P(),
        P(None, "head"),
        P(),
        P(),
        P("blk"),
    )
    return jax.shard_map(
        body, mesh=mesh, in_specs=placed, out_specs=P("blk", "head"), check_vma=False
    )
```

```python
import functools

import jax
import jax.numpy as jnp
from jax import lax
from jax.experimental import pallas as pl
from jax.experimental.pallas import tpu as pltpu
from jax.sharding import PartitionSpec as P

LANES = 128
SHORTEST = 17
WHOLE = 63
FLOOR = -1e30
F32 = jnp.float32
BF16 = jnp.bfloat16
I32 = jnp.int32


def cdiv(a, b):
    return -(-a // b)


def split_by(x, n):
    if n & (n - 1) == 0:
        return lax.shift_right_logical(x, n.bit_length() - 1), x & (n - 1)
    q = lax.div(x, n)
    return q, x - q * n


def iota(shape, dim):
    return lax.broadcasted_iota(I32, shape, dim)


def dot(a, b):
    return jnp.dot(a, b, preferred_element_type=F32)


def dot_exact(a, b):
    return jnp.dot(a, b, preferred_element_type=F32, precision=lax.Precision.HIGHEST)


def one_hot(mask):
    return jnp.where(mask, F32(1), F32(0)).astype(BF16)


def normalize(inputs, gain):
    mean_square = jnp.mean(inputs * inputs, axis=-1, keepdims=True)
    return inputs * lax.rsqrt(mean_square + 1e-05) * gain


class Sizes:
    def __init__(self, groups, cores, req_dev, pool_dev, block, heads, head_dim):
        self.groups, self.cores, self.req, self.pool = groups, cores, req_dev, pool_dev
        self.block, self.heads, self.dim = block, heads, head_dim
        self.total = groups * req_dev
        most = (pool_dev - 2) // SHORTEST + 2
        self.slot = cdiv(most, groups)
        self.slots = groups * self.slot
        self.width = heads * head_dim
        self.chunks = self.width // LANES
        self.wide = min(self.width, 2 * LANES)
        self.pair = LANES // head_dim


def deal(z, rows, out_ref, cores=1):
    for g in range(z.groups):
        part = rows[g * z.slot : (g + 1) * z.slot].astype(BF16)
        for core in range(cores):
            out_ref[g * cores + core] = part


def collect(z, ref, cores=1, core=0):
    return jnp.concatenate([ref[g * cores + core].astype(F32) for g in range(z.groups)], axis=0)


def place_rows(lengths, order, variate, step=512):
    total = order.shape[1]
    step = min(step, total)
    sub = iota((16, total), 0)
    table = jnp.where(
        sub == 0,
        lax.shift_right_logical(lengths, 6),
        jnp.where(sub == 1, lengths & 63, jnp.where(sub == 2, variate, 0)),
    )
    table = table.astype(F32).astype(BF16)
    request = iota((total, step), 0)
    found, sums = [], []
    for at in range(0, total, step):
        found.append(dot(table, one_hot(request == order[:, at : at + step])))
    ordered = jnp.concatenate(found, axis=1) if len(found) > 1 else found[0]
    ordered_low = ordered.astype(BF16)
    for at in range(0, total, step):
        before = one_hot(iota((at + step, step), 0) <= iota((at + step, step), 1) + at)
        sums.append(dot(ordered_low[:, : at + step], before))
    summed = jnp.concatenate(sums, axis=1) if len(sums) > 1 else sums[0]
    ends = summed[0:1] * 64.0 + summed[1:2]
    starts = ends - (ordered[0:1] * 64.0 + ordered[1:2])
    return starts, ends, ordered[2:3]


def fetch(pairs, sems):
    copies = [pltpu.make_async_copy(src, dst, sems.at[i]) for i, (src, dst) in enumerate(pairs)]
    for copy in copies:
        copy.start()
    return copies


def ask_kernel(z, lengths_hbm, order_hbm, variate_hbm, live_hbm, key_variate_hbm, bias_hbm, tokens_hbm,
               gain_hbm, w_query_hbm, ask_ref, rows_ref, facts_ref, home_ref,
               bias_ref, lengths_ref, order_ref, variate_ref, live_ref, key_variate_ref, tokens_ref,
               gain_ref, w_query_ref, sems):
    me = lax.axis_index("blk")
    copies = fetch(
        [
            (lengths_hbm, lengths_ref),
            (order_hbm, order_ref),
            (variate_hbm, variate_ref),
            (live_hbm, live_ref),
            (key_variate_hbm, key_variate_ref),
            (bias_hbm, bias_ref),
            (tokens_hbm, tokens_ref),
            (gain_hbm, gain_ref),
            (w_query_hbm, w_query_ref),
        ],
        sems,
    )
    for copy in copies[:6]:
        copy.wait()
    order = order_ref[...]
    starts, ends, variates = place_rows(lengths_ref[...], order, variate_ref[...])
    shape = (z.slots, z.total)
    place = iota(shape, 1)
    other, turn = split_by(iota((z.slots, 1), 0), z.slot)
    home_of, local = split_by(order, z.req)

    def choose(home, pool):
        low = (pool * z.pool).astype(F32)
        first = jnp.sum(jnp.where(ends <= low, F32(1), F32(0)), axis=1, keepdims=True)
        first = first.astype(I32) + turn * z.groups
        return (
            (home_of == home)
            & (starts < low + F32(z.pool))
            & (place >= first)
            & (place < first + z.groups)
        )

    mine = choose(me, other)
    row = jnp.sum(jnp.where(mine, local.astype(F32) + 1.0, F32(0)), axis=1, keepdims=True) - 1.0
    row = row.astype(I32)
    theirs = choose(other, jnp.full((1, 1), me, I32))
    low = (me * z.pool).astype(F32)
    begin = jnp.sum(jnp.where(theirs, starts - low, F32(0)), axis=1, keepdims=True)
    finish = jnp.sum(jnp.where(theirs, ends - low, F32(0)), axis=1, keepdims=True)
    kind = jnp.sum(jnp.where(theirs, variates, F32(0)), axis=1, keepdims=True)
    lane = iota((z.slots, LANES), 1)
    facts = jnp.where(lane == 0, begin, jnp.where(lane == 1, finish, kind))
    facts_ref[8:, 0:LANES] = facts
    home_ref[...] = jnp.broadcast_to(row, home_ref.shape)
    blocks = live_ref.shape[1]
    spread = one_hot(
        split_by(iota((blocks, z.pool), 1), z.block)[0] == iota((blocks, z.pool), 0)
    )
    live = jnp.broadcast_to(live_ref[...].astype(F32).astype(BF16), (16, blocks))
    kinds = jnp.where(dot(live, spread)[:1] > 0, key_variate_ref[...], -1)
    facts_ref[0:1, :] = kinds.astype(F32)
    facts_ref[1:3, 0 : z.heads] = bias_ref[...]

    for copy in copies[6:]:
        copy.wait()
    normed = normalize(tokens_ref[...].astype(F32), gain_ref[...]).astype(BF16)
    rows_ref[:, z.width :] = normed
    query = dot(normed, w_query_ref[...]).astype(BF16)
    rows_ref[:, : z.width] = query
    deal(z, dot(one_hot(row == iota((z.slots, z.req), 1)), query), ask_ref)


def pieces(z, columns):
    rows = columns[0].shape[0]
    lane = iota((rows, LANES), 1)
    full = jnp.zeros((rows, LANES), F32)
    for h, column in enumerate(columns):
        full = jnp.where((lane & (z.heads - 1)) == h, column, full)
    high = full.astype(BF16).astype(F32)
    rest = full - high
    middle = rest.astype(BF16).astype(F32)
    last = rest - middle
    n = z.heads
    return jnp.where(
        lane < n, high, jnp.where(lane < 2 * n, middle, jnp.where(lane < 3 * n, last, F32(0)))
    )


def hold_kernel(*refs):
    refs[-1][...] = jnp.zeros(refs[-1].shape, F32)


def own_kernel(z, after_ref, rows_ref, facts_ref, w_key_ref, w_value_ref, value_ref, stat_ref):
    del after_ref
    normed = rows_ref[:, z.width :]
    key_new = dot(normed, w_key_ref[...]).astype(BF16)
    product = rows_ref[:, : z.width].astype(F32) * key_new.astype(F32)
    columns = []
    for h in range(z.heads):
        c, inner = divmod(h, z.pair)
        part = product[:, c * LANES : (c + 1) * LANES]
        lane_head = split_by(iota(part.shape, 1), z.dim)[0]
        raw = jnp.sum(jnp.where(lane_head == inner, part, F32(0)), axis=1, keepdims=True)
        columns.append(raw * F32(z.dim**-0.5) + facts_ref[1:2, h : h + 1])
    stat_ref[...] = pieces(z, columns).astype(BF16)
    value_ref[...] = dot(normed, w_value_ref[...]).astype(BF16)


def attend_kernel(z, ask_ref, keys_ref, values_ref, facts_ref, after_ref, back_ref, done_ref):
    del after_ref
    done_ref[...] = jnp.zeros(done_ref.shape, F32)
    stacked = collect(z, ask_ref)
    begin, finish, kind = facts_ref[8:, 0:1], facts_ref[8:, 1:2], facts_ref[8:, 2:3]
    token = iota((z.slots, z.pool), 1).astype(F32)
    kinds = facts_ref[0:1, :]
    used = (token >= begin) & (token < finish) & (kinds >= 0)
    same = kinds == kind
    lane = split_by(iota((z.slots, z.wide), 1), z.dim)[0]
    many = z.wide // z.dim
    columns, parts = [], []
    for c in range(z.width // z.wide):
        chunk = slice(c * z.wide, (c + 1) * z.wide)
        asked = stacked[:, chunk]
        asked = (asked * F32(z.dim**-0.5)).astype(BF16)
        blocks = jnp.concatenate(
            [jnp.where(lane == i, asked, jnp.zeros_like(asked)) for i in range(many)], axis=0
        )
        score = lax.dot_general(
            blocks, keys_ref[:, chunk], (((1,), (1,)), ((), ())), preferred_element_type=F32
        )
        weights, scale = [], []
        for i in range(many):
            h = c * many + i
            one = score[i * z.slots : (i + 1) * z.slots]
            one = one + jnp.where(same, facts_ref[1:2, h : h + 1], facts_ref[2:3, h : h + 1])
            one = jnp.where(used, one, F32(FLOOR))
            top = jnp.maximum(jnp.max(one, axis=1, keepdims=True), F32(FLOOR * 0.1))
            weight = jnp.exp(one - top)
            total = jnp.sum(weight, axis=1, keepdims=True)
            some = total > 0
            safe = jnp.where(some, total, F32(1))
            columns.append(jnp.where(some, top + jnp.log(safe), F32(FLOOR)))
            scale.append(1.0 / safe)
            weights.append(weight.astype(BF16))
        summed = dot(jnp.concatenate(weights, axis=0), values_ref[:, chunk])
        part = summed[: z.slots] * scale[0]
        for i in range(1, many):
            part = jnp.where(lane == i, summed[i * z.slots : (i + 1) * z.slots] * scale[i], part)
        parts.append(part)
    parts.append(pieces(z, columns))
    deal(z, jnp.concatenate(parts, axis=1), back_ref, z.cores)


def merged(z, stacked, owner, value, stat):
    stat = jnp.concatenate([stacked[:, z.width :], stat], axis=0)
    rows = z.slots + z.req
    wide = z.heads * z.req
    head_at, _ = split_by(iota((LANES, wide), 1), z.req)
    from_lane = iota((LANES, wide), 0)
    spread = one_hot(((from_lane & (z.heads - 1)) == head_at) & (from_lane < 3 * z.heads))
    level = dot(stat, spread)
    _, request = split_by(iota((rows, wide), 1), z.req)
    match = owner == request
    level = jnp.where(match, level, F32(FLOOR))
    top = jnp.max(level, axis=0, keepdims=True)
    weight = jnp.where(match, jnp.exp(level - top), F32(0))
    weight = weight / jnp.sum(weight, axis=0, keepdims=True)
    high = weight.astype(BF16)
    low = (weight - high.astype(F32)).astype(BF16)
    held = jnp.concatenate([stacked[:, : z.width], value], axis=0)
    dims = (((0,), (0,)), ((), ()))
    summed = lax.dot_general(high, held, dims, preferred_element_type=F32)
    summed = summed + lax.dot_general(low, held, dims, preferred_element_type=F32)
    lane = split_by(iota((z.req, z.width), 1), z.dim)[0]
    attended = summed[: z.req]
    for h in range(1, z.heads):
        attended = jnp.where(lane == h, summed[h * z.req : (h + 1) * z.req], attended)
    return attended.astype(BF16)


def tail_kernel(z, steps, *refs):
    n = z.cores
    count = 4 + 3 * n
    given, gate_hbm, up_hbm, down_hbm = refs[:count], *refs[count : count + 3]
    refs = refs[count + 3 :]
    here_ref, away_refs = refs[0], refs[1:n]
    held, gate_ref, up_ref, down_ref, total_ref, sems = refs[n : n + count], *refs[n + count :]
    depth, units = gate_ref.shape[0] // steps, down_ref.shape[0] // steps
    deep = [slice(i * depth, (i + 1) * depth) for i in range(steps)]
    unit = [slice(i * units, (i + 1) * units) for i in range(steps)]
    pairs = list(zip(given, held))
    for at in deep:
        pairs += [(gate_hbm.at[at, :], gate_ref.at[at, :]), (up_hbm.at[at, :], up_ref.at[at, :])]
    pairs += [(down_hbm.at[at, :], down_ref.at[at, :]) for at in unit]
    copies = [pltpu.make_async_copy(src, dst, sems.at[i]) for i, (src, dst) in enumerate(pairs)]
    for copy in copies:
        copy.start()
    ready = 4 + 2 * n
    for copy in copies[:ready]:
        copy.wait()
    back_ref, home_ref, tokens_ref, gain_ref = held[:4]
    stats, values, outs = held[4 : 4 + n], held[4 + n : 4 + 2 * n], held[4 + 2 * n : 4 + 3 * n]
    me = lax.axis_index("head")
    owner = jnp.concatenate([home_ref[:, 0:1], iota((z.req, 1), 0)], axis=0)
    attended = []
    for i in range(n):
        core = lax.rem(me + i, n)
        stacked = collect(z, back_ref, n, core).astype(BF16)
        attended.append(merged(z, stacked, owner, values[i][...], stats[i][...]))
    for copy in copies[ready:count]:
        copy.wait()
    mixed = sum(dot(attended[i], outs[i][...]) for i in range(n))
    mixed = (tokens_ref[...].astype(F32) + mixed).astype(BF16).astype(F32)
    hidden_in = normalize(mixed, gain_ref[...]).astype(BF16)
    gate = upper = total = 0
    for i, at in enumerate(deep):
        for copy in copies[count + 2 * i : count + 2 * i + 2]:
            copy.wait()
        gate = gate + dot(hidden_in[:, at], gate_ref[at, :])
        upper = upper + dot(hidden_in[:, at], up_ref[at, :])
    hidden = (jax.nn.silu(gate) * upper).astype(BF16)
    for i, at in enumerate(unit):
        copies[count + 2 * steps + i].wait()
        total = total + dot(hidden[:, at], down_ref[at, :])
    width = mixed.shape[1] // n

    def block(i):
        return pl.ds(pl.multiple_of(lax.rem(me + i, n) * width, width), width)

    total_ref[0] = total
    total_ref[1] = mixed
    here_ref[...] = total_ref[0, :, block(0)] + total_ref[1, :, block(0)]
    for i in range(1, n):
        away_refs[i - 1][...] = total_ref[0, :, block(i)].astype(BF16)


VMEM = pl.BlockSpec(memory_space=pltpu.VMEM)
HBM = pl.BlockSpec(memory_space=pltpu.HBM)


def call(kernel, out, operands, specs, scratch=(), name=None, limit=16):
    return pl.pallas_call(
        kernel,
        out_shape=[jax.ShapeDtypeStruct(s, d) for s, d in out],
        in_specs=specs,
        out_specs=[VMEM] * len(out),
        scratch_shapes=list(scratch),
        compiler_params=pltpu.CompilerParams(vmem_limit_bytes=int(limit * 1024 * 1024)),
        cost_estimate=pl.CostEstimate(flops=10**10, bytes_accessed=10**7, transcendentals=0),
        name=name,
    )(*operands)


def from_core(x, shift):
    n = lax.axis_size("head")
    return lax.ppermute(x, "head", [((i + shift) % n, i) for i in range(n)])


def all_cores(x):
    return [x] + [from_core(x, i) for i in range(1, lax.axis_size("head"))]


def body(
    tokens,
    norm_gain,
    w_query,
    w_key,
    w_value,
    w_out,
    ffn_gain,
    w_gate,
    w_up,
    w_down,
    keys,
    values,
    key_variate,
    query_variate,
    bias,
    lengths,
    order,
    live_blocks,
):
    groups = lax.axis_size("blk")
    head_count = lax.axis_size("head")
    z = Sizes(
        groups,
        head_count,
        tokens.shape[0],
        keys.shape[0],
        keys.shape[0] // live_blocks.shape[0],
        bias.shape[1],
        w_query.shape[1] // bias.shape[1],
    )
    d_model = tokens.shape[1]
    width_local = d_model // head_count
    row = lambda x: x.reshape(1, -1)
    small = (row(lengths), row(order), row(query_variate), row(live_blocks), row(key_variate))
    operands = small + (bias, tokens, row(norm_gain), w_query)
    token = ((8, LANES), F32)
    ask, rows, facts, home = call(
        functools.partial(ask_kernel, z),
        [
            ((groups, z.slot, z.width), BF16),
            ((z.req, z.width + d_model), BF16),
            ((8 + z.slots, z.pool), F32),
            ((z.slots, LANES), I32),
        ],
        operands,
        [HBM] * len(operands),
        scratch=[pltpu.VMEM((2, z.heads), F32)]
        + [pltpu.VMEM(x.shape, x.dtype) for x in small + operands[6:]]
        + [pltpu.SemaphoreType.DMA((len(operands),))],
        name="ask",
        limit=WHOLE,
    )
    asked = lax.all_to_all(ask, "blk", 0, 0)
    (held,) = call(hold_kernel, [token], (facts, keys, values), [VMEM] * 3, name="hold")
    back, done = call(
        functools.partial(attend_kernel, z),
        [((groups * head_count, z.slot, z.width + LANES), BF16), token],
        (asked, keys, values, facts, held),
        [VMEM] * 5,
        name="attend",
    )
    returned = lax.all_to_all(back, ("blk", "head"), 0, 0)
    value_new, own = call(
        functools.partial(own_kernel, z),
        [((z.req, z.width), BF16), ((z.req, LANES), BF16)],
        (done, rows, facts, w_key, w_value),
        [VMEM] * 5,
        name="own",
    )
    w_out_after, _ = lax.optimization_barrier((w_out, held))
    outs = [w_out] + [from_core(w_out_after, i) for i in range(1, head_count)]
    given = (returned, home, tokens, row(ffn_gain), *all_cores(own), *all_cores(value_new), *outs)
    feed = (w_gate, w_up, w_down)
    steps = 8
    here, *away = call(
        functools.partial(tail_kernel, z, steps),
        [((z.req, width_local), F32)] + [((z.req, width_local), BF16)] * (head_count - 1),
        given + feed,
        [HBM] * (len(given) + 3),
        scratch=[pltpu.VMEM(x.shape, x.dtype) for x in given + feed]
        + [pltpu.VMEM((2, z.req, d_model), F32), pltpu.SemaphoreType.DMA((len(given) + 3 * steps,))],
        name="tail",
        limit=48,
    )
    for i, x in enumerate(away, 1):
        here = here + from_core(x, head_count - i).astype(F32)
    return here.astype(BF16)


def solution(mesh):
    placed = (
        P("blk", None),
        P(),
        P(None, "head"),
        P(None, "head"),
        P(None, "head"),
        P("head", None),
        P(),
        P(None, "head"),
        P(None, "head"),
        P("head", None),
        P("blk", "head"),
        P("blk", "head"),
        P("blk"),
        P(),
        P(None, "head"),
        P(),
        P(),
        P("blk"),
    )
    return jax.shard_map(
        body, mesh=mesh, in_specs=placed, out_specs=P("blk", "head"), check_vma=False
    )
```

```python
import functools

import jax
import jax.numpy as jnp
from jax import lax
from jax.experimental import pallas as pl
from jax.experimental.pallas import tpu as pltpu
from jax.sharding import PartitionSpec as P

LANES = 128
SHORTEST = 17
FLOOR = -1e30
STEPS = 4
DOWN_STEPS = 3
F32 = jnp.float32
BF16 = jnp.bfloat16
I32 = jnp.int32


def cdiv(a, b):
    return -(-a // b)


def split_by(x, n):
    if n & (n - 1) == 0:
        return lax.shift_right_logical(x, n.bit_length() - 1), x & (n - 1)
    q = lax.div(x, n)
    return q, x - q * n


def iota(shape, dim):
    return lax.broadcasted_iota(I32, shape, dim)


def dot(a, b):
    return jnp.dot(a, b, preferred_element_type=F32)


def dot_exact(a, b):
    return jnp.dot(a, b, preferred_element_type=F32, precision=lax.Precision.HIGHEST)


def one_hot(mask):
    return jnp.where(mask, F32(1), F32(0)).astype(BF16)


def normalize(inputs, gain):
    mean_square = jnp.mean(inputs * inputs, axis=-1, keepdims=True)
    return inputs * lax.rsqrt(mean_square + 1e-05) * gain


class Sizes:
    def __init__(self, groups, cores, req_dev, pool_dev, block, heads, head_dim):
        self.groups, self.cores, self.req, self.pool = groups, cores, req_dev, pool_dev
        self.block, self.heads, self.dim = block, heads, head_dim
        self.total = groups * req_dev
        most = (pool_dev - 2) // SHORTEST + 2
        self.slot = cdiv(most, groups)
        self.slots = groups * self.slot
        self.width = heads * head_dim
        self.chunks = self.width // LANES
        self.wide = min(self.width, 2 * LANES)
        self.pair = LANES // head_dim


def deal(z, rows, out_ref, cores=1):
    for g in range(z.groups):
        part = rows[g * z.slot : (g + 1) * z.slot].astype(BF16)
        for core in range(cores):
            out_ref[g * cores + core] = part


def collect(z, ref, cores=1, core=0):
    return jnp.concatenate([ref[g * cores + core].astype(F32) for g in range(z.groups)], axis=0)


def place_rows(lengths, order, variate, step=512):
    total = order.shape[1]
    step = min(step, total)
    sub = iota((16, total), 0)
    table = jnp.where(
        sub == 0,
        lax.shift_right_logical(lengths, 6),
        jnp.where(sub == 1, lengths & 63, jnp.where(sub == 2, variate, 0)),
    )
    table = table.astype(F32).astype(BF16)
    request = iota((total, step), 0)
    found, sums = [], []
    for at in range(0, total, step):
        found.append(dot(table, one_hot(request == order[:, at : at + step])))
    ordered = jnp.concatenate(found, axis=1) if len(found) > 1 else found[0]
    ordered_low = ordered.astype(BF16)
    for at in range(0, total, step):
        before = one_hot(iota((at + step, step), 0) <= iota((at + step, step), 1) + at)
        sums.append(dot(ordered_low[:, : at + step], before))
    summed = jnp.concatenate(sums, axis=1) if len(sums) > 1 else sums[0]
    ends = summed[0:1] * 64.0 + summed[1:2]
    starts = ends - (ordered[0:1] * 64.0 + ordered[1:2])
    return starts, ends, ordered[2:3]


def fetch(pairs, sems):
    copies = [pltpu.make_async_copy(src, dst, sems.at[i]) for i, (src, dst) in enumerate(pairs)]
    for copy in copies:
        copy.start()
    return copies


def ask_kernel(z, lengths_hbm, order_hbm, variate_hbm, live_hbm, key_variate_hbm, bias_hbm, tokens_hbm,
               gain_hbm, w_query_hbm, ask_ref, rows_ref, facts_ref, home_ref,
               bias_ref, lengths_ref, order_ref, variate_ref, live_ref, key_variate_ref, tokens_ref,
               gain_ref, w_query_ref, sems):
    me = lax.axis_index("blk")
    copies = fetch(
        [
            (lengths_hbm, lengths_ref),
            (order_hbm, order_ref),
            (variate_hbm, variate_ref),
            (live_hbm, live_ref),
            (key_variate_hbm, key_variate_ref),
            (bias_hbm, bias_ref),
            (tokens_hbm, tokens_ref),
            (gain_hbm, gain_ref),
            (w_query_hbm, w_query_ref),
        ],
        sems,
    )
    for copy in copies[:6]:
        copy.wait()
    order = order_ref[...]
    starts, ends, variates = place_rows(lengths_ref[...], order, variate_ref[...])
    shape = (z.slots, z.total)
    place = iota(shape, 1)
    other, turn = split_by(iota((z.slots, 1), 0), z.slot)
    home_of, local = split_by(order, z.req)

    def choose(home, pool):
        low = (pool * z.pool).astype(F32)
        first = jnp.sum(jnp.where(ends <= low, F32(1), F32(0)), axis=1, keepdims=True)
        first = first.astype(I32) + turn * z.groups
        return (
            (home_of == home)
            & (starts < low + F32(z.pool))
            & (place >= first)
            & (place < first + z.groups)
        )

    mine = choose(me, other)
    row = jnp.sum(jnp.where(mine, local.astype(F32) + 1.0, F32(0)), axis=1, keepdims=True) - 1.0
    row = row.astype(I32)
    theirs = choose(other, jnp.full((1, 1), me, I32))
    low = (me * z.pool).astype(F32)
    begin = jnp.sum(jnp.where(theirs, starts - low, F32(0)), axis=1, keepdims=True)
    finish = jnp.sum(jnp.where(theirs, ends - low, F32(0)), axis=1, keepdims=True)
    kind = jnp.sum(jnp.where(theirs, variates, F32(0)), axis=1, keepdims=True)
    lane = iota((z.slots, LANES), 1)
    facts = jnp.where(lane == 0, begin, jnp.where(lane == 1, finish, kind))
    facts_ref[8:, 0:LANES] = facts
    home_ref[...] = jnp.broadcast_to(row, home_ref.shape)
    blocks = live_ref.shape[1]
    spread = one_hot(
        split_by(iota((blocks, z.pool), 1), z.block)[0] == iota((blocks, z.pool), 0)
    )
    live = jnp.broadcast_to(live_ref[...].astype(F32).astype(BF16), (16, blocks))
    kinds = jnp.where(dot(live, spread)[:1] > 0, key_variate_ref[...], -1)
    facts_ref[0:1, :] = kinds.astype(F32)
    facts_ref[1:3, 0 : z.heads] = bias_ref[...]

    for copy in copies[6:]:
        copy.wait()
    normed = normalize(tokens_ref[...].astype(F32), gain_ref[...]).astype(BF16)
    rows_ref[:, z.width :] = normed
    query = dot(normed, w_query_ref[...]).astype(BF16)
    rows_ref[:, : z.width] = query
    deal(z, dot(one_hot(row == iota((z.slots, z.req), 1)), query), ask_ref)


def pieces(z, columns):
    rows = columns[0].shape[0]
    lane = iota((rows, LANES), 1)
    full = jnp.zeros((rows, LANES), F32)
    for h, column in enumerate(columns):
        full = jnp.where((lane & (z.heads - 1)) == h, column, full)
    high = full.astype(BF16).astype(F32)
    rest = full - high
    middle = rest.astype(BF16).astype(F32)
    last = rest - middle
    n = z.heads
    return jnp.where(
        lane < n, high, jnp.where(lane < 2 * n, middle, jnp.where(lane < 3 * n, last, F32(0)))
    )


def first_load_kernel(z, count, facts_ref, rows_ref, *refs):
    far, w_key_hbm, w_value_hbm = refs[:count], refs[count], refs[count + 1]
    near, own_ref, w_key_ref, w_value_ref, sems = refs[count + 2 : 2 * count + 2], *refs[2 * count + 2 :]
    copies = fetch([(w_key_hbm, w_key_ref), (w_value_hbm, w_value_ref), *zip(far, near)], sems)
    normed = rows_ref[:, z.width :]
    copies[0].wait()
    key_new = dot(normed, w_key_ref[...]).astype(BF16)
    product = rows_ref[:, : z.width].astype(F32) * key_new.astype(F32)
    columns = []
    for h in range(z.heads):
        c, inner = divmod(h, z.pair)
        part = product[:, c * LANES : (c + 1) * LANES]
        lane_head = split_by(iota(part.shape, 1), z.dim)[0]
        raw = jnp.sum(jnp.where(lane_head == inner, part, F32(0)), axis=1, keepdims=True)
        columns.append(raw * F32(z.dim**-0.5) + facts_ref[1:2, h : h + 1])
    own_ref[:, z.width :] = pieces(z, columns).astype(BF16)
    copies[1].wait()
    own_ref[:, : z.width] = dot(normed, w_value_ref[...]).astype(BF16)
    for copy in copies[2:]:
        copy.wait()


def second_load_kernel(count, after_ref, *refs):
    del after_ref
    down_hbm, down_ref, sems = refs[count], refs[-2], refs[-1]
    rows = down_ref.shape[0]
    pairs = list(zip(refs[:count], refs[count + 1 : 2 * count + 1]))
    pairs.append((down_hbm.at[down_hbm.shape[0] - rows :, :], down_ref))
    for copy in fetch(pairs, sems):
        copy.wait()


def attend_kernel(z, ask_ref, keys_ref, values_ref, facts_ref, back_ref, done_ref):
    done_ref[...] = jnp.zeros(done_ref.shape, F32)
    stacked = collect(z, ask_ref)
    begin, finish, kind = facts_ref[8:, 0:1], facts_ref[8:, 1:2], facts_ref[8:, 2:3]
    token = iota((z.slots, z.pool), 1).astype(F32)
    kinds = facts_ref[0:1, :]
    used = (token >= begin) & (token < finish) & (kinds >= 0)
    same = kinds == kind
    lane = split_by(iota((z.slots, z.wide), 1), z.dim)[0]
    many = z.wide // z.dim
    columns, parts = [], []
    for c in range(z.width // z.wide):
        chunk = slice(c * z.wide, (c + 1) * z.wide)
        asked = stacked[:, chunk]
        asked = (asked * F32(z.dim**-0.5)).astype(BF16)
        blocks = jnp.concatenate(
            [jnp.where(lane == i, asked, jnp.zeros_like(asked)) for i in range(many)], axis=0
        )
        score = lax.dot_general(
            blocks, keys_ref[:, chunk], (((1,), (1,)), ((), ())), preferred_element_type=F32
        )
        weights, scale = [], []
        for i in range(many):
            h = c * many + i
            one = score[i * z.slots : (i + 1) * z.slots]
            one = one + jnp.where(same, facts_ref[1:2, h : h + 1], facts_ref[2:3, h : h + 1])
            one = jnp.where(used, one, F32(FLOOR))
            top = jnp.maximum(jnp.max(one, axis=1, keepdims=True), F32(FLOOR * 0.1))
            weight = jnp.exp(one - top)
            total = jnp.sum(weight, axis=1, keepdims=True)
            some = total > 0
            safe = jnp.where(some, total, F32(1))
            columns.append(jnp.where(some, top + jnp.log(safe), F32(FLOOR)))
            scale.append(1.0 / safe)
            weights.append(weight.astype(BF16))
        summed = dot(jnp.concatenate(weights, axis=0), values_ref[:, chunk])
        part = summed[: z.slots] * scale[0]
        for i in range(1, many):
            part = jnp.where(lane == i, summed[i * z.slots : (i + 1) * z.slots] * scale[i], part)
        parts.append(part)
    parts.append(pieces(z, columns))
    deal(z, jnp.concatenate(parts, axis=1), back_ref, z.cores)


def merged(z, stacked, owner, value, stat):
    stat = jnp.concatenate([stacked[:, z.width :], stat], axis=0)
    rows = z.slots + z.req
    wide = z.heads * z.req
    head_at, _ = split_by(iota((LANES, wide), 1), z.req)
    from_lane = iota((LANES, wide), 0)
    spread = one_hot(((from_lane & (z.heads - 1)) == head_at) & (from_lane < 3 * z.heads))
    level = dot(stat, spread)
    _, request = split_by(iota((rows, wide), 1), z.req)
    match = owner == request
    level = jnp.where(match, level, F32(FLOOR))
    top = jnp.max(level, axis=0, keepdims=True)
    weight = jnp.where(match, jnp.exp(level - top), F32(0))
    weight = weight / jnp.sum(weight, axis=0, keepdims=True)
    high = weight.astype(BF16)
    held = jnp.concatenate([stacked[:, : z.width], value], axis=0)
    dims = (((0,), (0,)), ((), ()))
    summed = lax.dot_general(high, held, dims, preferred_element_type=F32)
    lane = split_by(iota((z.req, z.width), 1), z.dim)[0]
    attended = summed[: z.req]
    for h in range(1, z.heads):
        attended = jnp.where(lane == h, summed[h * z.req : (h + 1) * z.req], attended)
    return attended.astype(BF16)


def tail_kernel(z, steps, *refs):
    n = z.cores
    back_ref, home_ref, tokens_ref, gain_ref = refs[:4]
    owns, outs = refs[4 : 4 + n], refs[4 + n : 4 + 2 * n]
    kept_ref, gate_hbm, up_hbm, down_hbm, here_ref, *away_refs = refs[4 + 2 * n : 8 + 3 * n]
    gate_ref, up_ref, down_ref, total_ref, sems = refs[8 + 3 * n :]
    kept, streamed = kept_ref.shape[0], down_ref.shape[0]

    def cut(rows, count):
        return [slice(i * (rows // count), (i + 1) * (rows // count)) for i in range(count)]

    deep, unit = cut(gate_ref.shape[0], steps), cut(streamed, DOWN_STEPS)
    pairs = [(gate_hbm.at[at, :], gate_ref.at[at, :]) for at in deep]
    pairs += [(up_hbm.at[at, :], up_ref.at[at, :]) for at in deep]
    pairs += [(down_hbm.at[at, :], down_ref.at[at, :]) for at in unit]
    copies = fetch(pairs, sems)
    me = lax.axis_index("head")
    owner = jnp.concatenate([home_ref[:, 0:1], iota((z.req, 1), 0)], axis=0)
    attended = []
    for i in range(n):
        core = lax.rem(me + i, n)
        stacked = collect(z, back_ref, n, core).astype(BF16)
        attended.append(merged(z, stacked, owner, owns[i][:, : z.width], owns[i][:, z.width :]))
    mixed = sum(dot(attended[i], outs[i][...]) for i in range(n))
    mixed = (tokens_ref[...].astype(F32) + mixed).astype(BF16).astype(F32)
    hidden_in = normalize(mixed, gain_ref[...]).astype(BF16)
    gate = upper = 0
    for i, at in enumerate(deep):
        copies[i].wait()
        gate = gate + dot(hidden_in[:, at], gate_ref[at, :])
    gate = jax.nn.silu(gate)
    for i, at in enumerate(deep):
        copies[steps + i].wait()
        upper = upper + dot(hidden_in[:, at], up_ref[at, :])
    hidden = (gate * upper).astype(BF16)
    total = dot(hidden[:, streamed:], kept_ref[...])
    for i, at in enumerate(unit):
        copies[2 * steps + i].wait()
        total = total + dot(hidden[:, at], down_ref[at, :])
    width = mixed.shape[1] // n

    def block(i):
        return pl.ds(pl.multiple_of(lax.rem(me + i, n) * width, width), width)

    total_ref[0] = total
    total_ref[1] = mixed
    here_ref[...] = total_ref[0, :, block(0)] + total_ref[1, :, block(0)]
    for i in range(1, n):
        away_refs[i - 1][...] = total_ref[0, :, block(i)].astype(BF16)


VMEM = pl.BlockSpec(memory_space=pltpu.VMEM)
HBM = pl.BlockSpec(memory_space=pltpu.HBM)


def in_hbm(*arrays):
    return tuple(pltpu.with_memory_space_constraint(x, pltpu.HBM) for x in arrays)


def call(kernel, out, operands, specs, scratch=(), name=None, limit=16):
    return pl.pallas_call(
        kernel,
        out_shape=out,
        in_specs=specs,
        out_specs=[VMEM] * len(out),
        scratch_shapes=list(scratch),
        compiler_params=pltpu.CompilerParams(vmem_limit_bytes=int(limit * 1024 * 1024)),
        cost_estimate=pl.CostEstimate(flops=10**10, bytes_accessed=10**7, transcendentals=0),
        name=name,
    )(*operands)


def from_core(x, shift):
    n = lax.axis_size("head")
    return lax.ppermute(x, "head", [((i + shift) % n, i) for i in range(n)])


def all_cores(x):
    return [x] + [from_core(x, i) for i in range(1, lax.axis_size("head"))]


def body(
    tokens,
    norm_gain,
    w_query,
    w_key,
    w_value,
    w_out,
    ffn_gain,
    w_gate,
    w_up,
    w_down,
    keys,
    values,
    key_variate,
    query_variate,
    bias,
    lengths,
    order,
    live_blocks,
):
    groups = lax.axis_size("blk")
    head_count = lax.axis_size("head")
    z = Sizes(
        groups,
        head_count,
        tokens.shape[0],
        keys.shape[0],
        keys.shape[0] // live_blocks.shape[0],
        bias.shape[1],
        w_query.shape[1] // bias.shape[1],
    )
    d_model = tokens.shape[1]
    width_local = d_model // head_count
    row = lambda x: x.reshape(1, -1)
    small = (row(lengths), row(order), row(query_variate), row(live_blocks), row(key_variate))
    operands = small + (bias, tokens, row(norm_gain), w_query)
    ask, rows, facts, home = call(
        functools.partial(ask_kernel, z),
        [
            jax.ShapeDtypeStruct((groups, z.slot, z.width), BF16),
            pltpu.VMEM((z.req, z.width + d_model), BF16),
            pltpu.VMEM((8 + z.slots, z.pool), F32),
            pltpu.VMEM((z.slots, LANES), I32),
        ],
        in_hbm(*operands),
        [HBM] * len(operands),
        scratch=[pltpu.VMEM((2, z.heads), F32)]
        + [pltpu.VMEM(x.shape, x.dtype) for x in small + operands[6:]]
        + [pltpu.SemaphoreType.DMA((len(operands),))],
        name="ask",
    )
    asked = lax.all_to_all(ask, "blk", 0, 0)
    early = (keys, values)
    keys_near, values_near, own = call(
        functools.partial(first_load_kernel, z, len(early)),
        [pltpu.VMEM(x.shape, x.dtype) for x in early] + [pltpu.VMEM((z.req, z.width + LANES), BF16)],
        (facts, rows) + in_hbm(*early, w_key, w_value),
        [VMEM] * 2 + [HBM] * (len(early) + 2),
        scratch=[pltpu.VMEM(x.shape, x.dtype) for x in (w_key, w_value)]
        + [pltpu.SemaphoreType.DMA((len(early) + 2,))],
        name="first_load",
    )
    w_out_after, _ = lax.optimization_barrier((w_out, own))
    outs = [w_out] + [from_core(w_out_after, i) for i in range(1, head_count)]
    owns = all_cores(own)
    back, done = call(
        functools.partial(attend_kernel, z),
        [jax.ShapeDtypeStruct((groups * head_count, z.slot, z.width + LANES), BF16), pltpu.VMEM((8, LANES), F32)],
        (asked, keys_near, values_near, facts),
        [VMEM] * 4,
        name="attend",
    )
    returned = lax.all_to_all(back, ("blk", "head"), 0, 0)
    kept = w_down.shape[0] // 4
    late = (tokens, row(ffn_gain), *outs)
    tokens_near, gain_near, *outs_near, down_near = call(
        functools.partial(second_load_kernel, len(late)),
        [pltpu.VMEM(x.shape, x.dtype) for x in late] + [pltpu.VMEM((kept, d_model), BF16)],
        (done,) + in_hbm(*late, w_down),
        [VMEM] + [HBM] * (len(late) + 1),
        scratch=[pltpu.SemaphoreType.DMA((len(late) + 1,))],
        name="second_load",
    )
    given = (returned, home, tokens_near, gain_near, *owns, *outs_near, down_near)
    feed = (w_gate, w_up, w_down)
    here, *away = call(
        functools.partial(tail_kernel, z, STEPS),
        [pltpu.VMEM((z.req, width_local), F32)]
        + [pltpu.VMEM((z.req, width_local), BF16)] * (head_count - 1),
        given + in_hbm(*feed),
        [VMEM] * len(given) + [HBM] * 3,
        scratch=[pltpu.VMEM(x.shape, x.dtype) for x in feed[:2]]
        + [pltpu.VMEM((w_down.shape[0] - kept, d_model), BF16)]
        + [pltpu.VMEM((2, z.req, d_model), F32), pltpu.SemaphoreType.DMA((2 * STEPS + DOWN_STEPS,))],
        name="tail",
        limit=24,
    )
    for i, x in enumerate(away, 1):
        here = here + from_core(x, head_count - i).astype(F32)
    return here.astype(BF16)


def solution(mesh):
    placed = (
        P("blk", None),
        P(),
        P(None, "head"),
        P(None, "head"),
        P(None, "head"),
        P("head", None),
        P(),
        P(None, "head"),
        P(None, "head"),
        P("head", None),
        P("blk", "head"),
        P("blk", "head"),
        P("blk"),
        P(),
        P(None, "head"),
        P(),
        P(),
        P("blk"),
    )
    return jax.shard_map(
        body, mesh=mesh, in_specs=placed, out_specs=P("blk", "head"), check_vma=False
    )
```

```python
import functools

import jax
import jax.numpy as jnp
from jax import lax
from jax.experimental import pallas as pl
from jax.experimental.pallas import tpu as pltpu
from jax.sharding import PartitionSpec as P

LANES = 128
SHORTEST = 17
FLOOR = -1e30
STEPS = 4
DOWN_STEPS = 4
F32 = jnp.float32
BF16 = jnp.bfloat16
I32 = jnp.int32


def cdiv(a, b):
    return -(-a // b)


def split_by(x, n):
    if n & (n - 1) == 0:
        return lax.shift_right_logical(x, n.bit_length() - 1), x & (n - 1)
    q = lax.div(x, n)
    return q, x - q * n


def iota(shape, dim):
    return lax.broadcasted_iota(I32, shape, dim)


def dot(a, b):
    return jnp.dot(a, b, preferred_element_type=F32)


def dot_exact(a, b):
    return jnp.dot(a, b, preferred_element_type=F32, precision=lax.Precision.HIGHEST)


def one_hot(mask):
    return jnp.where(mask, F32(1), F32(0)).astype(BF16)


def normalize(inputs, gain):
    mean_square = jnp.mean(inputs * inputs, axis=-1, keepdims=True)
    return inputs * lax.rsqrt(mean_square + 1e-05) * gain


class Sizes:
    def __init__(self, groups, cores, req_dev, pool_dev, block, heads, head_dim):
        self.groups, self.cores, self.req, self.pool = groups, cores, req_dev, pool_dev
        self.block, self.heads, self.dim = block, heads, head_dim
        self.total = groups * req_dev
        most = (pool_dev - 2) // SHORTEST + 2
        self.slot = cdiv(most, groups)
        self.slots = groups * self.slot
        self.width = heads * head_dim
        self.chunks = self.width // LANES
        self.wide = min(self.width, 2 * LANES)
        self.pair = LANES // head_dim


def deal(z, rows, out_ref, cores=1):
    for g in range(z.groups):
        part = rows[g * z.slot : (g + 1) * z.slot].astype(BF16)
        for core in range(cores):
            out_ref[g * cores + core] = part


def collect(z, ref, cores=1, core=0):
    return jnp.concatenate([ref[g * cores + core].astype(F32) for g in range(z.groups)], axis=0)


def place_rows(lengths, order, variate, step=512):
    total = order.shape[1]
    step = min(step, total)
    sub = iota((16, total), 0)
    table = jnp.where(
        sub == 0,
        lax.shift_right_logical(lengths, 6),
        jnp.where(sub == 1, lengths & 63, jnp.where(sub == 2, variate, 0)),
    )
    table = table.astype(F32).astype(BF16)
    request = iota((total, step), 0)
    found, sums = [], []
    for at in range(0, total, step):
        found.append(dot(table, one_hot(request == order[:, at : at + step])))
    ordered = jnp.concatenate(found, axis=1) if len(found) > 1 else found[0]
    ordered_low = ordered.astype(BF16)
    for at in range(0, total, step):
        before = one_hot(iota((at + step, step), 0) <= iota((at + step, step), 1) + at)
        sums.append(dot(ordered_low[:, : at + step], before))
    summed = jnp.concatenate(sums, axis=1) if len(sums) > 1 else sums[0]
    ends = summed[0:1] * 64.0 + summed[1:2]
    starts = ends - (ordered[0:1] * 64.0 + ordered[1:2])
    return starts, ends, ordered[2:3]


def fetch(pairs, sems):
    copies = [pltpu.make_async_copy(src, dst, sems.at[i]) for i, (src, dst) in enumerate(pairs)]
    for copy in copies:
        copy.start()
    return copies


def choose(z, starts, ends, home_of, turn, home, pool):
    low = (pool * z.pool).astype(F32)
    first = jnp.sum(jnp.where(ends <= low, F32(1), F32(0)), axis=1, keepdims=True)
    first = first + (turn * z.groups).astype(F32)
    place = iota((z.slots, z.total), 1).astype(F32)
    return (
        (home_of == home)
        & (starts < low + F32(z.pool))
        & (place >= first)
        & (place < first + F32(z.groups))
    )


def ask_kernel(z, lengths_hbm, order_hbm, variate_hbm, tokens_hbm, gain_hbm, w_query_hbm, ask_ref, rows_ref,
               places_ref, home_ref, lengths_ref, order_ref, variate_ref, tokens_ref, gain_ref, w_query_ref,
               sems):
    me = lax.axis_index("blk")
    copies = fetch(
        [
            (lengths_hbm, lengths_ref),
            (order_hbm, order_ref),
            (variate_hbm, variate_ref),
            (tokens_hbm, tokens_ref),
            (gain_hbm, gain_ref),
            (w_query_hbm, w_query_ref),
        ],
        sems,
    )
    for copy in copies[:3]:
        copy.wait()
    order = order_ref[...]
    starts, ends, variates = place_rows(lengths_ref[...], order, variate_ref[...])
    home_of, local = split_by(order, z.req)
    places_ref[0:1, :] = starts
    places_ref[1:2, :] = ends
    places_ref[2:3, :] = variates
    places_ref[3:4, :] = home_of.astype(F32)
    other, turn = split_by(iota((z.slots, 1), 0), z.slot)
    mine = choose(z, starts, ends, home_of, turn, me, other)
    row = jnp.sum(jnp.where(mine, local.astype(F32) + 1.0, F32(0)), axis=1, keepdims=True) - 1.0
    row = row.astype(I32)
    home_ref[...] = jnp.broadcast_to(row, home_ref.shape)

    for copy in copies[3:]:
        copy.wait()
    normed = normalize(tokens_ref[...].astype(F32), gain_ref[...]).astype(BF16)
    rows_ref[:, z.width :] = normed
    query = dot(normed, w_query_ref[...]).astype(BF16)
    rows_ref[:, : z.width] = query
    deal(z, dot(one_hot(row == iota((z.slots, z.req), 1)), query), ask_ref)


def slot_facts(z, places_ref, live, key_variate, bias, facts_ref):
    me = lax.axis_index("blk")
    starts, ends, variates = places_ref[0:1, :], places_ref[1:2, :], places_ref[2:3, :]
    home_of = places_ref[3:4, :].astype(I32)
    other, turn = split_by(iota((z.slots, 1), 0), z.slot)
    theirs = choose(z, starts, ends, home_of, turn, other, jnp.full((1, 1), me, I32))
    low = (me * z.pool).astype(F32)
    begin = jnp.sum(jnp.where(theirs, starts - low, F32(0)), axis=1, keepdims=True)
    finish = jnp.sum(jnp.where(theirs, ends - low, F32(0)), axis=1, keepdims=True)
    kind = jnp.sum(jnp.where(theirs, variates, F32(0)), axis=1, keepdims=True)
    lane = iota((z.slots, LANES), 1)
    facts_ref[8:, 0:LANES] = jnp.where(lane == 0, begin, jnp.where(lane == 1, finish, kind))
    blocks = live.shape[1]
    spread = one_hot(
        split_by(iota((blocks, z.pool), 1), z.block)[0] == iota((blocks, z.pool), 0)
    )
    live = jnp.broadcast_to(live.astype(F32).astype(BF16), (16, blocks))
    kinds = jnp.where(dot(live, spread)[:1] > 0, key_variate, -1)
    facts_ref[0:1, :] = kinds.astype(F32)
    facts_ref[1:3, 0 : z.heads] = bias


def pieces(z, columns):
    rows = columns[0].shape[0]
    lane = iota((rows, LANES), 1)
    full = jnp.zeros((rows, LANES), F32)
    for h, column in enumerate(columns):
        full = jnp.where((lane & (z.heads - 1)) == h, column, full)
    high = full.astype(BF16).astype(F32)
    rest = full - high
    middle = rest.astype(BF16).astype(F32)
    last = rest - middle
    n = z.heads
    return jnp.where(
        lane < n, high, jnp.where(lane < 2 * n, middle, jnp.where(lane < 3 * n, last, F32(0)))
    )


def first_load_kernel(z, count, places_ref, rows_ref, *refs):
    far, small = refs[:count], refs[count : count + 5]
    near, (facts_ref, own_ref) = refs[count + 5 : 2 * count + 5], refs[2 * count + 5 : 2 * count + 7]
    held, sems = refs[2 * count + 7 : -1], refs[-1]
    copies = fetch([*zip(small, held), *zip(far, near)], sems)
    live_ref, key_variate_ref, bias_ref, w_key_ref, w_value_ref = held
    for copy in copies[:3]:
        copy.wait()
    slot_facts(z, places_ref, live_ref[...], key_variate_ref[...], bias_ref[...], facts_ref)
    normed = rows_ref[:, z.width :]
    copies[3].wait()
    key_new = dot(normed, w_key_ref[...]).astype(BF16)
    product = rows_ref[:, : z.width].astype(F32) * key_new.astype(F32)
    columns = []
    for h in range(z.heads):
        c, inner = divmod(h, z.pair)
        part = product[:, c * LANES : (c + 1) * LANES]
        lane_head = split_by(iota(part.shape, 1), z.dim)[0]
        raw = jnp.sum(jnp.where(lane_head == inner, part, F32(0)), axis=1, keepdims=True)
        columns.append(raw * F32(z.dim**-0.5) + bias_ref[0:1, h : h + 1])
    own_ref[:, z.width :] = pieces(z, columns).astype(BF16)
    copies[4].wait()
    own_ref[:, : z.width] = dot(normed, w_value_ref[...]).astype(BF16)
    for copy in copies[5:]:
        copy.wait()


def core_columns(ref, shift, cores):
    width = ref.shape[-1] // cores
    core = lax.rem(lax.axis_index("head") + shift, cores)
    return ref.at[:, pl.ds(pl.multiple_of(core * width, width), width)]


def second_load_kernel(z, count, after_ref, *refs):
    del after_ref
    pairs = list(zip(refs[:count], refs[count + 1 : 2 * count + 1]))
    pairs.append((core_columns(refs[count], 0, z.cores), refs[-2]))
    for copy in fetch(pairs, refs[-1]):
        copy.wait()


def attend_kernel(z, ask_ref, keys_ref, values_ref, facts_ref, back_ref, done_ref):
    done_ref[...] = jnp.zeros(done_ref.shape, F32)
    stacked = collect(z, ask_ref)
    begin, finish, kind = facts_ref[8:, 0:1], facts_ref[8:, 1:2], facts_ref[8:, 2:3]
    token = iota((z.slots, z.pool), 1).astype(F32)
    kinds = facts_ref[0:1, :]
    used = (token >= begin) & (token < finish) & (kinds >= 0)
    same = kinds == kind
    lane = split_by(iota((z.slots, z.wide), 1), z.dim)[0]
    many = z.wide // z.dim
    columns, parts = [], []
    for c in range(z.width // z.wide):
        chunk = slice(c * z.wide, (c + 1) * z.wide)
        asked = stacked[:, chunk]
        asked = (asked * F32(z.dim**-0.5)).astype(BF16)
        blocks = jnp.concatenate(
            [jnp.where(lane == i, asked, jnp.zeros_like(asked)) for i in range(many)], axis=0
        )
        score = lax.dot_general(
            blocks, keys_ref[:, chunk], (((1,), (1,)), ((), ())), preferred_element_type=F32
        )
        weights, scale = [], []
        for i in range(many):
            h = c * many + i
            one = score[i * z.slots : (i + 1) * z.slots]
            one = one + jnp.where(same, facts_ref[1:2, h : h + 1], facts_ref[2:3, h : h + 1])
            one = jnp.where(used, one, F32(FLOOR))
            top = jnp.maximum(jnp.max(one, axis=1, keepdims=True), F32(FLOOR * 0.1))
            weight = jnp.exp(one - top)
            total = jnp.sum(weight, axis=1, keepdims=True)
            some = total > 0
            safe = jnp.where(some, total, F32(1))
            columns.append(jnp.where(some, top + jnp.log(safe), F32(FLOOR)))
            scale.append(1.0 / safe)
            weights.append(weight.astype(BF16))
        summed = dot(jnp.concatenate(weights, axis=0), values_ref[:, chunk])
        part = summed[: z.slots] * scale[0]
        for i in range(1, many):
            part = jnp.where(lane == i, summed[i * z.slots : (i + 1) * z.slots] * scale[i], part)
        parts.append(part)
    parts.append(pieces(z, columns))
    deal(z, jnp.concatenate(parts, axis=1), back_ref, z.cores)


def merged(z, stacked, owner, value, stat):
    stat = jnp.concatenate([stacked[:, z.width :], stat], axis=0)
    rows = z.slots + z.req
    wide = z.heads * z.req
    head_at, _ = split_by(iota((LANES, wide), 1), z.req)
    from_lane = iota((LANES, wide), 0)
    spread = one_hot(((from_lane & (z.heads - 1)) == head_at) & (from_lane < 3 * z.heads))
    level = dot(stat, spread)
    _, request = split_by(iota((rows, wide), 1), z.req)
    match = owner == request
    level = jnp.where(match, level, F32(FLOOR))
    top = jnp.max(level, axis=0, keepdims=True)
    weight = jnp.where(match, jnp.exp(level - top), F32(0))
    weight = weight / jnp.sum(weight, axis=0, keepdims=True)
    high = weight.astype(BF16)
    held = jnp.concatenate([stacked[:, : z.width], value], axis=0)
    dims = (((0,), (0,)), ((), ()))
    summed = lax.dot_general(high, held, dims, preferred_element_type=F32)
    lane = split_by(iota((z.req, z.width), 1), z.dim)[0]
    attended = summed[: z.req]
    for h in range(1, z.heads):
        attended = jnp.where(lane == h, summed[h * z.req : (h + 1) * z.req], attended)
    return attended.astype(BF16)


def tail_kernel(z, *refs):
    n = z.cores
    back_ref, home_ref, tokens_ref, gain_ref = refs[:4]
    owns, out_ref, refs = refs[4 : 4 + n], refs[4 + n], refs[5 + n :]
    out_hbms, (gate_hbm, up_hbm, down_hbm), refs = refs[: n - 1], refs[n - 1 : n + 2], refs[n + 2 :]
    hidden_ref, here_ref, away_refs, refs = refs[0], refs[1], refs[2 : n + 1], refs[n + 1 :]
    out_refs, (gate_ref, up_ref), refs = refs[: n - 1], refs[n - 1 : n + 1], refs[n + 1 :]
    down_refs, mixed_ref, sems = refs[: n - 1], refs[n - 1], refs[n]

    def cut(rows, count):
        return [slice(i * (rows // count), (i + 1) * (rows // count)) for i in range(count)]

    deep, unit = cut(gate_ref.shape[0], STEPS), cut(down_hbm.shape[0], DOWN_STEPS)
    pairs = list(zip(out_hbms, out_refs))
    pairs += [(gate_hbm.at[at, :], gate_ref.at[at, :]) for at in deep]
    pairs += [(up_hbm.at[at, :], up_ref.at[at, :]) for at in deep]
    for i in range(1, n):
        columns = core_columns(down_hbm, i, n)
        pairs += [(columns.at[at, :], down_refs[i - 1].at[at, :]) for at in unit]
    copies = iter(fetch(pairs, sems))
    me = lax.axis_index("head")
    owner = jnp.concatenate([home_ref[:, 0:1], iota((z.req, 1), 0)], axis=0)
    attended = []
    for i in range(n):
        core = lax.rem(me + i, n)
        stacked = collect(z, back_ref, n, core).astype(BF16)
        attended.append(merged(z, stacked, owner, owns[i][:, : z.width], owns[i][:, z.width :]))
    mixed = dot(attended[0], out_ref[...])
    for i in range(1, n):
        next(copies).wait()
        mixed = mixed + dot(attended[i], out_refs[i - 1][...])
    mixed = (tokens_ref[...].astype(F32) + mixed).astype(BF16).astype(F32)
    mixed_ref[...] = mixed
    here_ref[...] = core_columns(mixed_ref, 0, n)[...]
    hidden_in = normalize(mixed, gain_ref[...]).astype(BF16)
    gate = upper = 0
    for at in deep:
        next(copies).wait()
        gate = gate + dot(hidden_in[:, at], gate_ref[at, :])
    gate = jax.nn.silu(gate)
    for at in deep:
        next(copies).wait()
        upper = upper + dot(hidden_in[:, at], up_ref[at, :])
    hidden = (gate * upper).astype(BF16)
    hidden_ref[...] = hidden
    for away_ref, down_ref in zip(away_refs, down_refs):
        total = 0
        for at in unit:
            next(copies).wait()
            total = total + dot(hidden[:, at], down_ref[at, :])
        away_ref[...] = total.astype(BF16)


def finish_kernel(hidden_ref, mixed_ref, down_ref, here_ref):
    here_ref[...] = mixed_ref[...] + dot(hidden_ref[...], down_ref[...])


VMEM = pl.BlockSpec(memory_space=pltpu.VMEM)
HBM = pl.BlockSpec(memory_space=pltpu.HBM)


def in_hbm(*arrays):
    return tuple(pltpu.with_memory_space_constraint(x, pltpu.HBM) for x in arrays)


def call(kernel, out, operands, specs, scratch=(), name=None, limit=16):
    return pl.pallas_call(
        kernel,
        out_shape=out,
        in_specs=specs,
        out_specs=[VMEM] * len(out),
        scratch_shapes=list(scratch),
        compiler_params=pltpu.CompilerParams(vmem_limit_bytes=int(limit * 1024 * 1024)),
        cost_estimate=pl.CostEstimate(flops=10**10, bytes_accessed=10**7, transcendentals=0),
        name=name,
    )(*operands)


def from_core(x, shift):
    n = lax.axis_size("head")
    return lax.ppermute(x, "head", [((i + shift) % n, i) for i in range(n)])


def all_cores(x):
    return [x] + [from_core(x, i) for i in range(1, lax.axis_size("head"))]


def body(
    tokens,
    norm_gain,
    w_query,
    w_key,
    w_value,
    w_out,
    ffn_gain,
    w_gate,
    w_up,
    w_down,
    keys,
    values,
    key_variate,
    query_variate,
    bias,
    lengths,
    order,
    live_blocks,
):
    groups = lax.axis_size("blk")
    head_count = lax.axis_size("head")
    z = Sizes(
        groups,
        head_count,
        tokens.shape[0],
        keys.shape[0],
        keys.shape[0] // live_blocks.shape[0],
        bias.shape[1],
        w_query.shape[1] // bias.shape[1],
    )
    d_model = tokens.shape[1]
    width_local = d_model // head_count
    row = lambda x: x.reshape(1, -1)
    operands = (row(lengths), row(order), row(query_variate), tokens, row(norm_gain), w_query)
    ask, rows, places, home = call(
        functools.partial(ask_kernel, z),
        [
            jax.ShapeDtypeStruct((groups, z.slot, z.width), BF16),
            pltpu.VMEM((z.req, z.width + d_model), BF16),
            pltpu.VMEM((8, z.total), F32),
            pltpu.VMEM((z.slots, LANES), I32),
        ],
        in_hbm(*operands),
        [HBM] * len(operands),
        scratch=[pltpu.VMEM(x.shape, x.dtype) for x in operands]
        + [pltpu.SemaphoreType.DMA((len(operands),))],
        name="ask",
    )
    asked = lax.all_to_all(ask, "blk", 0, 0)
    early, small = (keys, values), (row(live_blocks), row(key_variate), bias, w_key, w_value)
    keys_near, values_near, facts, own = call(
        functools.partial(first_load_kernel, z, len(early)),
        [pltpu.VMEM(x.shape, x.dtype) for x in early]
        + [pltpu.VMEM((8 + z.slots, z.pool), F32), pltpu.VMEM((z.req, z.width + LANES), BF16)],
        (places, rows) + in_hbm(*early, *small),
        [VMEM] * 2 + [HBM] * (len(early) + len(small)),
        scratch=[pltpu.VMEM(x.shape, x.dtype) for x in small]
        + [pltpu.SemaphoreType.DMA((len(early) + len(small),))],
        name="first_load",
    )
    w_out_after, _ = lax.optimization_barrier((w_out, own))
    outs = [w_out] + [from_core(w_out_after, i) for i in range(1, head_count)]
    owns = all_cores(own)
    back, done = call(
        functools.partial(attend_kernel, z),
        [jax.ShapeDtypeStruct((groups * head_count, z.slot, z.width + LANES), BF16), pltpu.VMEM((8, LANES), F32)],
        (asked, keys_near, values_near, facts),
        [VMEM] * 4,
        name="attend",
    )
    returned = lax.all_to_all(back, ("blk", "head"), 0, 0)
    late = (tokens, row(ffn_gain), w_out)
    units = w_down.shape[0]
    tokens_near, gain_near, out_near, down_near = call(
        functools.partial(second_load_kernel, z, len(late)),
        [pltpu.VMEM(x.shape, x.dtype) for x in late] + [pltpu.VMEM((units, width_local), BF16)],
        (done,) + in_hbm(*late, w_down),
        [VMEM] + [HBM] * (len(late) + 1),
        scratch=[pltpu.SemaphoreType.DMA((len(late) + 1,))],
        name="second_load",
    )
    given = (returned, home, tokens_near, gain_near, *owns, out_near)
    streamed = (*outs[1:], w_gate, w_up)
    hidden, here, *away = call(
        functools.partial(tail_kernel, z),
        [pltpu.VMEM((z.req, units), BF16), pltpu.VMEM((z.req, width_local), F32)]
        + [pltpu.VMEM((z.req, width_local), BF16)] * (head_count - 1),
        given + in_hbm(*streamed, w_down),
        [VMEM] * len(given) + [HBM] * (len(streamed) + 1),
        scratch=[pltpu.VMEM(x.shape, x.dtype) for x in streamed]
        + [pltpu.VMEM((units, width_local), BF16)] * (head_count - 1)
        + [
            pltpu.VMEM((z.req, d_model), F32),
            pltpu.SemaphoreType.DMA((head_count - 1 + 2 * STEPS + DOWN_STEPS * (head_count - 1),)),
        ],
        name="tail",
        limit=24,
    )
    arrived = [from_core(x, head_count - i) for i, x in enumerate(away, 1)]
    (here,) = call(
        finish_kernel,
        [pltpu.VMEM((z.req, width_local), F32)],
        (hidden, here, down_near),
        [VMEM] * 3,
        name="finish",
    )
    for x in arrived:
        here = here + x.astype(F32)
    return here.astype(BF16)


def solution(mesh):
    placed = (
        P("blk", None),
        P(),
        P(None, "head"),
        P(None, "head"),
        P(None, "head"),
        P("head", None),
        P(),
        P(None, "head"),
        P(None, "head"),
        P("head", None),
        P("blk", "head"),
        P("blk", "head"),
        P("blk"),
        P(),
        P(None, "head"),
        P(),
        P(),
        P("blk"),
    )
    return jax.shard_map(
        body, mesh=mesh, in_specs=placed, out_specs=P("blk", "head"), check_vma=False
    )
```

```python
import functools

import jax
import jax.numpy as jnp
from jax import lax
from jax.experimental import pallas as pl
from jax.experimental.pallas import tpu as pltpu
from jax.sharding import PartitionSpec as P

LANES = 128
SHORTEST = 17
FLOOR = -1e30
STEPS = 4
DOWN_STEPS = 4
F32 = jnp.float32
BF16 = jnp.bfloat16
I32 = jnp.int32


def cdiv(a, b):
    return -(-a // b)


def split_by(x, n):
    if n & (n - 1) == 0:
        return lax.shift_right_logical(x, n.bit_length() - 1), x & (n - 1)
    q = lax.div(x, n)
    return q, x - q * n


def iota(shape, dim):
    return lax.broadcasted_iota(I32, shape, dim)


def dot(a, b):
    return jnp.dot(a, b, preferred_element_type=F32)


def dot_exact(a, b):
    return jnp.dot(a, b, preferred_element_type=F32, precision=lax.Precision.HIGHEST)


def one_hot(mask):
    return jnp.where(mask, F32(1), F32(0)).astype(BF16)


def normalize(inputs, gain):
    mean_square = jnp.mean(inputs * inputs, axis=-1, keepdims=True)
    return inputs * lax.rsqrt(mean_square + 1e-05) * gain


class Sizes:
    def __init__(self, groups, cores, req_dev, pool_dev, block, heads, head_dim):
        self.groups, self.cores, self.req, self.pool = groups, cores, req_dev, pool_dev
        self.block, self.heads, self.dim = block, heads, head_dim
        self.total = groups * req_dev
        most = (pool_dev - 2) // SHORTEST + 2
        self.slot = cdiv(most, groups)
        self.slots = groups * self.slot
        self.width = heads * head_dim
        self.chunks = self.width // LANES
        self.wide = min(self.width, 2 * LANES)
        self.pair = LANES // head_dim


def deal(z, rows, out_ref, cores=1):
    for g in range(z.groups):
        part = rows[g * z.slot : (g + 1) * z.slot].astype(BF16)
        for core in range(cores):
            out_ref[g * cores + core] = part


def collect(z, ref, cores=1, core=0):
    return jnp.concatenate([ref[g * cores + core].astype(F32) for g in range(z.groups)], axis=0)


def place_rows(lengths, order, variate, step=512):
    total = order.shape[1]
    step = min(step, total)
    sub = iota((16, total), 0)
    table = jnp.where(
        sub == 0,
        lax.shift_right_logical(lengths, 6),
        jnp.where(sub == 1, lengths & 63, jnp.where(sub == 2, variate, 0)),
    )
    table = table.astype(F32).astype(BF16)
    request = iota((total, step), 0)
    found, sums = [], []
    for at in range(0, total, step):
        found.append(dot(table, one_hot(request == order[:, at : at + step])))
    ordered = jnp.concatenate(found, axis=1) if len(found) > 1 else found[0]
    ordered_low = ordered.astype(BF16)
    for at in range(0, total, step):
        before = one_hot(iota((at + step, step), 0) <= iota((at + step, step), 1) + at)
        sums.append(dot(ordered_low[:, : at + step], before))
    summed = jnp.concatenate(sums, axis=1) if len(sums) > 1 else sums[0]
    ends = summed[0:1] * 64.0 + summed[1:2]
    starts = ends - (ordered[0:1] * 64.0 + ordered[1:2])
    return starts, ends, ordered[2:3]


def fetch(pairs, sems):
    copies = [pltpu.make_async_copy(src, dst, sems.at[i]) for i, (src, dst) in enumerate(pairs)]
    for copy in copies:
        copy.start()
    return copies


def choose(z, starts, ends, home_of, turn, home, pool):
    low = (pool * z.pool).astype(F32)
    first = jnp.sum(jnp.where(ends <= low, F32(1), F32(0)), axis=1, keepdims=True)
    first = first + (turn * z.groups).astype(F32)
    place = iota((z.slots, z.total), 1).astype(F32)
    return (
        (home_of == home)
        & (starts < low + F32(z.pool))
        & (place >= first)
        & (place < first + F32(z.groups))
    )


def ask_kernel(z, lengths_hbm, order_hbm, variate_hbm, tokens_hbm, gain_hbm, w_query_hbm, ask_ref, rows_ref,
               places_ref, home_ref, lengths_ref, order_ref, variate_ref, tokens_ref, gain_ref, w_query_ref,
               sems):
    me = lax.axis_index("blk")
    half = w_query_hbm.shape[0] // 2
    copies = fetch(
        [
            (lengths_hbm, lengths_ref),
            (order_hbm, order_ref),
            (variate_hbm, variate_ref),
            (tokens_hbm, tokens_ref),
            (gain_hbm, gain_ref),
            (w_query_hbm.at[:half, :], w_query_ref.at[:half, :]),
            (w_query_hbm.at[half:, :], w_query_ref.at[half:, :]),
        ],
        sems,
    )
    for copy in copies[:3]:
        copy.wait()
    order = order_ref[...]
    starts, ends, variates = place_rows(lengths_ref[...], order, variate_ref[...])
    home_of, local = split_by(order, z.req)
    places_ref[0:1, :] = starts
    places_ref[1:2, :] = ends
    places_ref[2:3, :] = variates
    places_ref[3:4, :] = home_of.astype(F32)
    other, turn = split_by(iota((z.slots, 1), 0), z.slot)
    mine = choose(z, starts, ends, home_of, turn, me, other)
    row = jnp.sum(jnp.where(mine, local.astype(F32) + 1.0, F32(0)), axis=1, keepdims=True) - 1.0
    row = row.astype(I32)
    home_ref[...] = jnp.broadcast_to(row, home_ref.shape)

    for copy in copies[3:]:
        copy.wait()
    normed = normalize(tokens_ref[...].astype(F32), gain_ref[...]).astype(BF16)
    rows_ref[:, z.width :] = normed
    query = dot(normed, w_query_ref[...]).astype(BF16)
    rows_ref[:, : z.width] = query
    deal(z, dot(one_hot(row == iota((z.slots, z.req), 1)), query), ask_ref)


def slot_facts(z, places_ref, live, key_variate, bias, facts_ref):
    me = lax.axis_index("blk")
    starts, ends, variates = places_ref[0:1, :], places_ref[1:2, :], places_ref[2:3, :]
    home_of = places_ref[3:4, :].astype(I32)
    other, turn = split_by(iota((z.slots, 1), 0), z.slot)
    theirs = choose(z, starts, ends, home_of, turn, other, jnp.full((1, 1), me, I32))
    low = (me * z.pool).astype(F32)
    begin = jnp.sum(jnp.where(theirs, starts - low, F32(0)), axis=1, keepdims=True)
    finish = jnp.sum(jnp.where(theirs, ends - low, F32(0)), axis=1, keepdims=True)
    kind = jnp.sum(jnp.where(theirs, variates, F32(0)), axis=1, keepdims=True)
    blocks = live.shape[1]
    spread = one_hot(
        split_by(iota((blocks, z.pool), 1), z.block)[0] == iota((blocks, z.pool), 0)
    )
    live = jnp.broadcast_to(live.astype(F32).astype(BF16), (16, blocks))
    kinds = jnp.where(dot(live, spread)[:1] > 0, key_variate, -1)
    kinds = kinds.astype(F32)
    token = iota((z.slots, z.pool), 1).astype(F32)
    used = (token >= begin) & (token < finish) & (kinds >= 0)
    facts_ref[: z.slots, :] = jnp.where(kinds == kind, F32(1), F32(0))
    facts_ref[z.slots : 2 * z.slots, :] = jnp.where(used, F32(0), F32(FLOOR))
    facts_ref[2 * z.slots : 2 * z.slots + 2, 0 : z.heads] = bias


def pieces(z, columns):
    rows = columns[0].shape[0]
    lane = iota((rows, LANES), 1)
    full = jnp.zeros((rows, LANES), F32)
    for h, column in enumerate(columns):
        full = jnp.where((lane & (z.heads - 1)) == h, column, full)
    high = full.astype(BF16).astype(F32)
    rest = full - high
    middle = rest.astype(BF16).astype(F32)
    last = rest - middle
    n = z.heads
    return jnp.where(
        lane < n, high, jnp.where(lane < 2 * n, middle, jnp.where(lane < 3 * n, last, F32(0)))
    )


def first_load_kernel(z, count, places_ref, rows_ref, *refs):
    far, small = refs[:count], refs[count : count + 5]
    near, (facts_ref, own_ref) = refs[count + 5 : 2 * count + 5], refs[2 * count + 5 : 2 * count + 7]
    held, sems = refs[2 * count + 7 : -1], refs[-1]
    copies = fetch([*zip(small, held), *zip(far, near)], sems)
    live_ref, key_variate_ref, bias_ref, w_key_ref, w_value_ref = held
    for copy in copies[:3]:
        copy.wait()
    slot_facts(z, places_ref, live_ref[...], key_variate_ref[...], bias_ref[...], facts_ref)
    normed = rows_ref[:, z.width :]
    copies[3].wait()
    key_new = dot(normed, w_key_ref[...]).astype(BF16)
    product = rows_ref[:, : z.width].astype(F32) * key_new.astype(F32)
    columns = []
    for h in range(z.heads):
        c, inner = divmod(h, z.pair)
        part = product[:, c * LANES : (c + 1) * LANES]
        lane_head = split_by(iota(part.shape, 1), z.dim)[0]
        raw = jnp.sum(jnp.where(lane_head == inner, part, F32(0)), axis=1, keepdims=True)
        columns.append(raw * F32(z.dim**-0.5) + bias_ref[0:1, h : h + 1])
    own_ref[:, z.width :] = pieces(z, columns).astype(BF16)
    copies[4].wait()
    own_ref[:, : z.width] = dot(normed, w_value_ref[...]).astype(BF16)
    for copy in copies[5:]:
        copy.wait()


def core_columns(ref, shift, cores):
    width = ref.shape[-1] // cores
    core = lax.rem(lax.axis_index("head") + shift, cores)
    return ref.at[:, pl.ds(pl.multiple_of(core * width, width), width)]


def second_load_kernel(z, count, after_ref, *refs):
    del after_ref
    pairs = list(zip(refs[:count], refs[count + 1 : 2 * count + 1]))
    pairs.append((core_columns(refs[count], 0, z.cores), refs[-2]))
    for copy in fetch(pairs, refs[-1]):
        copy.wait()


def attend_kernel(z, ask_ref, keys_ref, values_ref, facts_ref, back_ref, done_ref):
    done_ref[...] = jnp.zeros(done_ref.shape, F32)
    stacked = collect(z, ask_ref)
    same, unused = facts_ref[: z.slots, :], facts_ref[z.slots : 2 * z.slots, :]
    bias = facts_ref[2 * z.slots : 2 * z.slots + 2, 0 : z.heads]
    lane = split_by(iota((z.slots, z.wide), 1), z.dim)[0]
    many = z.wide // z.dim
    columns, parts = [], []
    for c in range(z.width // z.wide):
        chunk = slice(c * z.wide, (c + 1) * z.wide)
        asked = stacked[:, chunk]
        asked = (asked * F32(z.dim**-0.5)).astype(BF16)
        blocks = jnp.concatenate(
            [jnp.where(lane == i, asked, jnp.zeros_like(asked)) for i in range(many)], axis=0
        )
        score = lax.dot_general(
            blocks, keys_ref[:, chunk], (((1,), (1,)), ((), ())), preferred_element_type=F32
        )
        weights, scale = [], []
        for i in range(many):
            h = c * many + i
            one = score[i * z.slots : (i + 1) * z.slots]
            one = one + (same * (bias[0:1, h : h + 1] - bias[1:2, h : h + 1]) + unused)
            top = jnp.maximum(jnp.max(one, axis=1, keepdims=True), F32(FLOOR * 0.1))
            weight = jnp.exp(one - top)
            total = jnp.sum(weight, axis=1, keepdims=True)
            some = total > 0
            safe = jnp.where(some, total, F32(1))
            columns.append(jnp.where(some, top + bias[1:2, h : h + 1] + jnp.log(safe), F32(FLOOR)))
            scale.append(1.0 / safe)
            weights.append(weight.astype(BF16))
        summed = dot(jnp.concatenate(weights, axis=0), values_ref[:, chunk])
        part = summed[: z.slots] * scale[0]
        for i in range(1, many):
            part = jnp.where(lane == i, summed[i * z.slots : (i + 1) * z.slots] * scale[i], part)
        parts.append(part)
    parts.append(pieces(z, columns))
    deal(z, jnp.concatenate(parts, axis=1), back_ref, z.cores)


def merged(z, stacked, owner, value, stat):
    stat = jnp.concatenate([stacked[:, z.width :], stat], axis=0)
    rows = z.slots + z.req
    wide = z.heads * z.req
    head_at, _ = split_by(iota((LANES, wide), 1), z.req)
    from_lane = iota((LANES, wide), 0)
    spread = one_hot(((from_lane & (z.heads - 1)) == head_at) & (from_lane < 3 * z.heads))
    level = dot(stat, spread)
    _, request = split_by(iota((rows, wide), 1), z.req)
    match = owner == request
    level = jnp.where(match, level, F32(FLOOR))
    top = jnp.max(level, axis=0, keepdims=True)
    weight = jnp.where(match, jnp.exp(level - top), F32(0))
    weight = weight / jnp.sum(weight, axis=0, keepdims=True)
    high = weight.astype(BF16)
    held = jnp.concatenate([stacked[:, : z.width], value], axis=0)
    dims = (((0,), (0,)), ((), ()))
    summed = lax.dot_general(high, held, dims, preferred_element_type=F32)
    lane = split_by(iota((z.req, z.width), 1), z.dim)[0]
    attended = summed[: z.req]
    for h in range(1, z.heads):
        attended = jnp.where(lane == h, summed[h * z.req : (h + 1) * z.req], attended)
    return attended.astype(BF16)


def tail_kernel(z, *refs):
    n = z.cores
    back_ref, home_ref, tokens_ref, gain_ref = refs[:4]
    owns, out_ref, refs = refs[4 : 4 + n], refs[4 + n], refs[5 + n :]
    out_hbms, (gate_hbm, up_hbm, down_hbm), refs = refs[: n - 1], refs[n - 1 : n + 2], refs[n + 2 :]
    hidden_ref, here_ref, away_refs, refs = refs[0], refs[1], refs[2 : n + 1], refs[n + 1 :]
    out_refs, (gate_ref, up_ref), refs = refs[: n - 1], refs[n - 1 : n + 1], refs[n + 1 :]
    down_refs, mixed_ref, sems = refs[: n - 1], refs[n - 1], refs[n]

    def cut(rows, count):
        return [slice(i * (rows // count), (i + 1) * (rows // count)) for i in range(count)]

    deep, unit = cut(gate_ref.shape[0], STEPS), cut(down_hbm.shape[0], DOWN_STEPS)
    pairs = list(zip(out_hbms, out_refs))
    pairs += [(gate_hbm.at[at, :], gate_ref.at[at, :]) for at in deep]
    pairs += [(up_hbm.at[at, :], up_ref.at[at, :]) for at in deep]
    for i in range(1, n):
        columns = core_columns(down_hbm, i, n)
        pairs += [(columns.at[at, :], down_refs[i - 1].at[at, :]) for at in unit]
    copies = iter(fetch(pairs, sems))
    me = lax.axis_index("head")
    owner = jnp.concatenate([home_ref[:, 0:1], iota((z.req, 1), 0)], axis=0)
    attended = []
    for i in range(n):
        core = lax.rem(me + i, n)
        stacked = collect(z, back_ref, n, core).astype(BF16)
        attended.append(merged(z, stacked, owner, owns[i][:, : z.width], owns[i][:, z.width :]))
    mixed = dot(attended[0], out_ref[...])
    for i in range(1, n):
        next(copies).wait()
        mixed = mixed + dot(attended[i], out_refs[i - 1][...])
    mixed = (tokens_ref[...].astype(F32) + mixed).astype(BF16).astype(F32)
    mixed_ref[...] = mixed
    here_ref[...] = core_columns(mixed_ref, 0, n)[...]
    hidden_in = normalize(mixed, gain_ref[...]).astype(BF16)
    gate = upper = 0
    for at in deep:
        next(copies).wait()
        gate = gate + dot(hidden_in[:, at], gate_ref[at, :])
    gate = jax.nn.silu(gate)
    for at in deep:
        next(copies).wait()
        upper = upper + dot(hidden_in[:, at], up_ref[at, :])
    hidden = (gate * upper).astype(BF16)
    hidden_ref[...] = hidden
    for away_ref, down_ref in zip(away_refs, down_refs):
        total = 0
        for at in unit:
            next(copies).wait()
            total = total + dot(hidden[:, at], down_ref[at, :])
        away_ref[...] = total.astype(BF16)


def finish_kernel(hidden_ref, mixed_ref, down_ref, here_ref):
    here_ref[...] = mixed_ref[...] + dot(hidden_ref[...], down_ref[...])


VMEM = pl.BlockSpec(memory_space=pltpu.VMEM)
HBM = pl.BlockSpec(memory_space=pltpu.HBM)


def in_hbm(*arrays):
    return tuple(pltpu.with_memory_space_constraint(x, pltpu.HBM) for x in arrays)


def call(kernel, out, operands, specs, scratch=(), name=None, limit=16):
    return pl.pallas_call(
        kernel,
        out_shape=out,
        in_specs=specs,
        out_specs=[VMEM] * len(out),
        scratch_shapes=list(scratch),
        compiler_params=pltpu.CompilerParams(vmem_limit_bytes=int(limit * 1024 * 1024)),
        cost_estimate=pl.CostEstimate(flops=10**10, bytes_accessed=10**7, transcendentals=0),
        name=name,
    )(*operands)


def from_core(x, shift):
    n = lax.axis_size("head")
    return lax.ppermute(x, "head", [((i + shift) % n, i) for i in range(n)])


def all_cores(x):
    return [x] + [from_core(x, i) for i in range(1, lax.axis_size("head"))]


def body(
    tokens,
    norm_gain,
    w_query,
    w_key,
    w_value,
    w_out,
    ffn_gain,
    w_gate,
    w_up,
    w_down,
    keys,
    values,
    key_variate,
    query_variate,
    bias,
    lengths,
    order,
    live_blocks,
):
    groups = lax.axis_size("blk")
    head_count = lax.axis_size("head")
    z = Sizes(
        groups,
        head_count,
        tokens.shape[0],
        keys.shape[0],
        keys.shape[0] // live_blocks.shape[0],
        bias.shape[1],
        w_query.shape[1] // bias.shape[1],
    )
    d_model = tokens.shape[1]
    width_local = d_model // head_count
    row = lambda x: x.reshape(1, -1)
    operands = (row(lengths), row(order), row(query_variate), tokens, row(norm_gain), w_query)
    ask, rows, places, home = call(
        functools.partial(ask_kernel, z),
        [
            jax.ShapeDtypeStruct((groups, z.slot, z.width), BF16),
            pltpu.VMEM((z.req, z.width + d_model), BF16),
            pltpu.VMEM((8, z.total), F32),
            pltpu.VMEM((z.slots, LANES), I32),
        ],
        in_hbm(*operands),
        [HBM] * len(operands),
        scratch=[pltpu.VMEM(x.shape, x.dtype) for x in operands]
        + [pltpu.SemaphoreType.DMA((len(operands) + 1,))],
        name="ask",
    )
    asked = lax.all_to_all(ask, "blk", 0, 0)
    early, small = (keys, values), (row(live_blocks), row(key_variate), bias, w_key, w_value)
    keys_near, values_near, facts, own = call(
        functools.partial(first_load_kernel, z, len(early)),
        [pltpu.VMEM(x.shape, x.dtype) for x in early]
        + [pltpu.VMEM((8 + 2 * z.slots, z.pool), F32), pltpu.VMEM((z.req, z.width + LANES), BF16)],
        (places, rows) + in_hbm(*early, *small),
        [VMEM] * 2 + [HBM] * (len(early) + len(small)),
        scratch=[pltpu.VMEM(x.shape, x.dtype) for x in small]
        + [pltpu.SemaphoreType.DMA((len(early) + len(small),))],
        name="first_load",
    )
    w_out_after, _ = lax.optimization_barrier((w_out, own))
    outs = [w_out] + [from_core(w_out_after, i) for i in range(1, head_count)]
    owns = all_cores(own)
    back, done = call(
        functools.partial(attend_kernel, z),
        [jax.ShapeDtypeStruct((groups * head_count, z.slot, z.width + LANES), BF16), pltpu.VMEM((8, LANES), F32)],
        (asked, keys_near, values_near, facts),
        [VMEM] * 4,
        name="attend",
    )
    returned = lax.all_to_all(back, ("blk", "head"), 0, 0)
    late = (tokens, row(ffn_gain), w_out)
    units = w_down.shape[0]
    tokens_near, gain_near, out_near, down_near = call(
        functools.partial(second_load_kernel, z, len(late)),
        [pltpu.VMEM(x.shape, x.dtype) for x in late] + [pltpu.VMEM((units, width_local), BF16)],
        (done,) + in_hbm(*late, w_down),
        [VMEM] + [HBM] * (len(late) + 1),
        scratch=[pltpu.SemaphoreType.DMA((len(late) + 1,))],
        name="second_load",
    )
    given = (returned, home, tokens_near, gain_near, *owns, out_near)
    streamed = (*outs[1:], w_gate, w_up)
    hidden, here, *away = call(
        functools.partial(tail_kernel, z),
        [pltpu.VMEM((z.req, units), BF16), pltpu.VMEM((z.req, width_local), F32)]
        + [pltpu.VMEM((z.req, width_local), BF16)] * (head_count - 1),
        given + in_hbm(*streamed, w_down),
        [VMEM] * len(given) + [HBM] * (len(streamed) + 1),
        scratch=[pltpu.VMEM(x.shape, x.dtype) for x in streamed]
        + [pltpu.VMEM((units, width_local), BF16)] * (head_count - 1)
        + [
            pltpu.VMEM((z.req, d_model), F32),
            pltpu.SemaphoreType.DMA((head_count - 1 + 2 * STEPS + DOWN_STEPS * (head_count - 1),)),
        ],
        name="tail",
        limit=24,
    )
    arrived = [from_core(x, head_count - i) for i, x in enumerate(away, 1)]
    (here,) = call(
        finish_kernel,
        [pltpu.VMEM((z.req, width_local), F32)],
        (hidden, here, down_near),
        [VMEM] * 3,
        name="finish",
    )
    for x in arrived:
        here = here + x.astype(F32)
    return here.astype(BF16)


def solution(mesh):
    placed = (
        P("blk", None),
        P(),
        P(None, "head"),
        P(None, "head"),
        P(None, "head"),
        P("head", None),
        P(),
        P(None, "head"),
        P(None, "head"),
        P("head", None),
        P("blk", "head"),
        P("blk", "head"),
        P("blk"),
        P(),
        P(None, "head"),
        P(),
        P(),
        P("blk"),
    )
    return jax.shard_map(
        body, mesh=mesh, in_specs=placed, out_specs=P("blk", "head"), check_vma=False
    )
```

```python
import functools

import jax
import jax.numpy as jnp
from jax import lax
from jax.experimental import pallas as pl
from jax.experimental.pallas import tpu as pltpu
from jax.sharding import PartitionSpec as P

LANES = 128
SHORTEST = 17
FLOOR = -1e30
STEPS = 4
DOWN_STEPS = 4
F32 = jnp.float32
BF16 = jnp.bfloat16
I32 = jnp.int32


def cdiv(a, b):
    return -(-a // b)


def split_by(x, n):
    if n & (n - 1) == 0:
        return lax.shift_right_logical(x, n.bit_length() - 1), x & (n - 1)
    q = lax.div(x, n)
    return q, x - q * n


def iota(shape, dim):
    return lax.broadcasted_iota(I32, shape, dim)


def dot(a, b):
    return jnp.dot(a, b, preferred_element_type=F32)


def dot_exact(a, b):
    return jnp.dot(a, b, preferred_element_type=F32, precision=lax.Precision.HIGHEST)


def one_hot(mask):
    return jnp.where(mask, F32(1), F32(0)).astype(BF16)


def normalize(inputs, gain):
    mean_square = jnp.mean(inputs * inputs, axis=-1, keepdims=True)
    return inputs * lax.rsqrt(mean_square + 1e-05) * gain


class Sizes:
    def __init__(self, groups, cores, req_dev, pool_dev, block, heads, head_dim):
        self.groups, self.cores, self.req, self.pool = groups, cores, req_dev, pool_dev
        self.block, self.heads, self.dim = block, heads, head_dim
        self.total = groups * req_dev
        most = (pool_dev - 2) // SHORTEST + 2
        self.slot = cdiv(most, groups)
        self.slots = groups * self.slot
        self.width = heads * head_dim
        self.chunks = self.width // LANES
        self.wide = min(self.width, 2 * LANES)
        self.pair = LANES // head_dim


def deal(z, rows, out_ref, cores=1):
    for g in range(z.groups):
        part = rows[g * z.slot : (g + 1) * z.slot].astype(BF16)
        for core in range(cores):
            out_ref[g * cores + core] = part


def collect(z, ref, cores=1, core=0):
    return jnp.concatenate([ref[g * cores + core].astype(F32) for g in range(z.groups)], axis=0)


def place_rows(lengths, order, step=512):
    total = order.shape[1]
    step = min(step, total)
    sub = iota((16, total), 0)
    table = jnp.where(
        sub == 0,
        lax.shift_right_logical(lengths, 6),
        jnp.where(sub == 1, lengths & 63, 0),
    )
    table = table.astype(F32).astype(BF16)
    request = iota((total, step), 0)
    found, sums = [], []
    for at in range(0, total, step):
        found.append(dot(table, one_hot(request == order[:, at : at + step])))
    ordered = jnp.concatenate(found, axis=1) if len(found) > 1 else found[0]
    ordered_low = ordered.astype(BF16)
    for at in range(0, total, step):
        before = one_hot(iota((at + step, step), 0) <= iota((at + step, step), 1) + at)
        sums.append(dot(ordered_low[:, : at + step], before))
    summed = jnp.concatenate(sums, axis=1) if len(sums) > 1 else sums[0]
    ends = summed[0:1] * 64.0 + summed[1:2]
    starts = ends - (ordered[0:1] * 64.0 + ordered[1:2])
    return starts, ends


def fetch(pairs, sems):
    copies = [pltpu.make_async_copy(src, dst, sems.at[i]) for i, (src, dst) in enumerate(pairs)]
    for copy in copies:
        copy.start()
    return copies


def choose(z, starts, ends, home_of, turn, home, pool):
    low = (pool * z.pool).astype(F32)
    first = jnp.sum(jnp.where(ends <= low, F32(1), F32(0)), axis=1, keepdims=True)
    first = first + (turn * z.groups).astype(F32)
    place = iota((z.slots, z.total), 1).astype(F32)
    return (
        (home_of == home)
        & (starts < low + F32(z.pool))
        & (place >= first)
        & (place < first + F32(z.groups))
    )


def ask_kernel(z, lengths_hbm, order_hbm, tokens_hbm, gain_hbm, w_query_hbm, ask_ref, rows_ref,
               places_ref, home_ref, lengths_ref, order_ref, tokens_ref, gain_ref, w_query_ref,
               sems):
    me = lax.axis_index("blk")
    half = w_query_hbm.shape[0] // 2
    copies = fetch(
        [
            (lengths_hbm, lengths_ref),
            (order_hbm, order_ref),
            (tokens_hbm, tokens_ref),
            (gain_hbm, gain_ref),
            (w_query_hbm.at[:half, :], w_query_ref.at[:half, :]),
            (w_query_hbm.at[half:, :], w_query_ref.at[half:, :]),
        ],
        sems,
    )
    for copy in copies[:2]:
        copy.wait()
    order = order_ref[...]
    starts, ends = place_rows(lengths_ref[...], order)
    home_of, local = split_by(order, z.req)
    places_ref[0:1, :] = starts
    places_ref[1:2, :] = ends
    places_ref[2:3, :] = order.astype(F32)
    other, turn = split_by(iota((z.slots, 1), 0), z.slot)
    mine = choose(z, starts, ends, home_of, turn, me, other)
    row = jnp.sum(jnp.where(mine, local.astype(F32) + 1.0, F32(0)), axis=1, keepdims=True) - 1.0
    row = row.astype(I32)
    home_ref[...] = jnp.broadcast_to(row, home_ref.shape)

    for copy in copies[2:]:
        copy.wait()
    normed = normalize(tokens_ref[...].astype(F32), gain_ref[...]).astype(BF16)
    rows_ref[:, z.width :] = normed
    query = dot(normed, w_query_ref[...]).astype(BF16)
    rows_ref[:, : z.width] = query
    deal(z, dot(one_hot(row == iota((z.slots, z.req), 1)), query), ask_ref)


def slot_facts(z, places_ref, variate, live, key_variate, bias, facts_ref):
    me = lax.axis_index("blk")
    starts, ends, order = places_ref[0:1, :], places_ref[1:2, :], places_ref[2:3, :]
    home_of, _ = split_by(order.astype(I32), z.req)
    other, turn = split_by(iota((z.slots, 1), 0), z.slot)
    theirs = choose(z, starts, ends, home_of, turn, other, jnp.full((1, 1), me, I32))
    low = (me * z.pool).astype(F32)
    begin = jnp.sum(jnp.where(theirs, starts - low, F32(0)), axis=1, keepdims=True)
    finish = jnp.sum(jnp.where(theirs, ends - low, F32(0)), axis=1, keepdims=True)
    request = jnp.sum(jnp.where(theirs, order, F32(0)), axis=1, keepdims=True).astype(I32)
    its = request == iota((z.slots, z.total), 1)
    kind = jnp.sum(jnp.where(its, variate.astype(F32), F32(0)), axis=1, keepdims=True)
    blocks = live.shape[1]
    spread = one_hot(
        split_by(iota((blocks, z.pool), 1), z.block)[0] == iota((blocks, z.pool), 0)
    )
    live = jnp.broadcast_to(live.astype(F32).astype(BF16), (16, blocks))
    kinds = jnp.where(dot(live, spread)[:1] > 0, key_variate, -1)
    kinds = kinds.astype(F32)
    token = iota((z.slots, z.pool), 1).astype(F32)
    used = (token >= begin) & (token < finish) & (kinds >= 0)
    facts_ref[: z.slots, :] = jnp.where(kinds == kind, F32(1), F32(0))
    facts_ref[z.slots : 2 * z.slots, :] = jnp.where(used, F32(0), F32(FLOOR))
    facts_ref[2 * z.slots : 2 * z.slots + 2, 0 : z.heads] = bias


def pieces(z, columns):
    rows = columns[0].shape[0]
    lane = iota((rows, LANES), 1)
    full = jnp.zeros((rows, LANES), F32)
    for h, column in enumerate(columns):
        full = jnp.where((lane & (z.heads - 1)) == h, column, full)
    high = full.astype(BF16).astype(F32)
    rest = full - high
    middle = rest.astype(BF16).astype(F32)
    last = rest - middle
    n = z.heads
    return jnp.where(
        lane < n, high, jnp.where(lane < 2 * n, middle, jnp.where(lane < 3 * n, last, F32(0)))
    )


def first_load_kernel(z, count, places_ref, rows_ref, *refs):
    far, small = refs[:count], refs[count : count + 6]
    near, (facts_ref, own_ref) = refs[count + 6 : 2 * count + 6], refs[2 * count + 6 : 2 * count + 8]
    held, sems = refs[2 * count + 8 : -1], refs[-1]
    copies = fetch([*zip(small, held), *zip(far, near)], sems)
    variate_ref, live_ref, key_variate_ref, bias_ref, w_key_ref, w_value_ref = held
    for copy in copies[:4]:
        copy.wait()
    slot_facts(z, places_ref, variate_ref[...], live_ref[...], key_variate_ref[...], bias_ref[...], facts_ref)
    normed = rows_ref[:, z.width :]
    copies[4].wait()
    key_new = dot(normed, w_key_ref[...]).astype(BF16)
    product = rows_ref[:, : z.width].astype(F32) * key_new.astype(F32)
    columns = []
    for h in range(z.heads):
        c, inner = divmod(h, z.pair)
        part = product[:, c * LANES : (c + 1) * LANES]
        lane_head = split_by(iota(part.shape, 1), z.dim)[0]
        raw = jnp.sum(jnp.where(lane_head == inner, part, F32(0)), axis=1, keepdims=True)
        columns.append(raw * F32(z.dim**-0.5) + bias_ref[0:1, h : h + 1])
    own_ref[:, z.width :] = pieces(z, columns).astype(BF16)
    copies[5].wait()
    own_ref[:, : z.width] = dot(normed, w_value_ref[...]).astype(BF16)
    for copy in copies[6:]:
        copy.wait()


def core_columns(ref, shift, cores):
    width = ref.shape[-1] // cores
    core = lax.rem(lax.axis_index("head") + shift, cores)
    return ref.at[:, pl.ds(pl.multiple_of(core * width, width), width)]


def second_load_kernel(z, count, after_ref, *refs):
    del after_ref
    pairs = list(zip(refs[:count], refs[count + 1 : 2 * count + 1]))
    pairs.append((core_columns(refs[count], 0, z.cores), refs[-2]))
    for copy in fetch(pairs, refs[-1]):
        copy.wait()


def attend_kernel(z, ask_ref, keys_ref, values_ref, facts_ref, back_ref, done_ref):
    done_ref[...] = jnp.zeros(done_ref.shape, F32)
    stacked = collect(z, ask_ref)
    same, unused = facts_ref[: z.slots, :], facts_ref[z.slots : 2 * z.slots, :]
    bias = facts_ref[2 * z.slots : 2 * z.slots + 2, 0 : z.heads]
    lane = split_by(iota((z.slots, z.wide), 1), z.dim)[0]
    many = z.wide // z.dim
    columns, parts = [], []
    for c in range(z.width // z.wide):
        chunk = slice(c * z.wide, (c + 1) * z.wide)
        asked = stacked[:, chunk]
        asked = (asked * F32(z.dim**-0.5)).astype(BF16)
        blocks = jnp.concatenate(
            [jnp.where(lane == i, asked, jnp.zeros_like(asked)) for i in range(many)], axis=0
        )
        score = lax.dot_general(
            blocks, keys_ref[:, chunk], (((1,), (1,)), ((), ())), preferred_element_type=F32
        )
        weights, scale = [], []
        for i in range(many):
            h = c * many + i
            one = score[i * z.slots : (i + 1) * z.slots]
            one = one + (same * (bias[0:1, h : h + 1] - bias[1:2, h : h + 1]) + unused)
            top = jnp.maximum(jnp.max(one, axis=1, keepdims=True), F32(FLOOR * 0.1))
            weight = jnp.exp(one - top)
            total = jnp.sum(weight, axis=1, keepdims=True)
            some = total > 0
            safe = jnp.where(some, total, F32(1))
            columns.append(jnp.where(some, top + bias[1:2, h : h + 1] + jnp.log(safe), F32(FLOOR)))
            scale.append(1.0 / safe)
            weights.append(weight.astype(BF16))
        summed = dot(jnp.concatenate(weights, axis=0), values_ref[:, chunk])
        part = summed[: z.slots] * scale[0]
        for i in range(1, many):
            part = jnp.where(lane == i, summed[i * z.slots : (i + 1) * z.slots] * scale[i], part)
        parts.append(part)
    parts.append(pieces(z, columns))
    deal(z, jnp.concatenate(parts, axis=1), back_ref, z.cores)


def merged(z, stacked, owner, value, stat):
    stat = jnp.concatenate([stacked[:, z.width :], stat], axis=0)
    rows = z.slots + z.req
    wide = z.heads * z.req
    head_at, _ = split_by(iota((LANES, wide), 1), z.req)
    from_lane = iota((LANES, wide), 0)
    spread = one_hot(((from_lane & (z.heads - 1)) == head_at) & (from_lane < 3 * z.heads))
    level = dot(stat, spread)
    _, request = split_by(iota((rows, wide), 1), z.req)
    match = owner == request
    level = jnp.where(match, level, F32(FLOOR))
    top = jnp.max(level, axis=0, keepdims=True)
    weight = jnp.where(match, jnp.exp(level - top), F32(0))
    weight = weight / jnp.sum(weight, axis=0, keepdims=True)
    high = weight.astype(BF16)
    held = jnp.concatenate([stacked[:, : z.width], value], axis=0)
    dims = (((0,), (0,)), ((), ()))
    summed = lax.dot_general(high, held, dims, preferred_element_type=F32)
    lane = split_by(iota((z.req, z.width), 1), z.dim)[0]
    attended = summed[: z.req]
    for h in range(1, z.heads):
        attended = jnp.where(lane == h, summed[h * z.req : (h + 1) * z.req], attended)
    return attended.astype(BF16)


def tail_kernel(z, *refs):
    n = z.cores
    back_ref, home_ref, tokens_ref, gain_ref = refs[:4]
    owns, out_ref, refs = refs[4 : 4 + n], refs[4 + n], refs[5 + n :]
    out_hbms, (gate_hbm, up_hbm, down_hbm), refs = refs[: n - 1], refs[n - 1 : n + 2], refs[n + 2 :]
    hidden_ref, here_ref, away_refs, refs = refs[0], refs[1], refs[2 : n + 1], refs[n + 1 :]
    out_refs, (gate_ref, up_ref), refs = refs[: n - 1], refs[n - 1 : n + 1], refs[n + 1 :]
    down_refs, mixed_ref, sems = refs[: n - 1], refs[n - 1], refs[n]

    def cut(rows, count):
        return [slice(i * (rows // count), (i + 1) * (rows // count)) for i in range(count)]

    deep, unit = cut(gate_ref.shape[0], STEPS), cut(down_hbm.shape[0], DOWN_STEPS)
    pairs = list(zip(out_hbms, out_refs))
    pairs += [(gate_hbm.at[at, :], gate_ref.at[at, :]) for at in deep]
    pairs += [(up_hbm.at[at, :], up_ref.at[at, :]) for at in deep]
    for i in range(1, n):
        columns = core_columns(down_hbm, i, n)
        pairs += [(columns.at[at, :], down_refs[i - 1].at[at, :]) for at in unit]
    copies = iter(fetch(pairs, sems))
    me = lax.axis_index("head")
    owner = jnp.concatenate([home_ref[:, 0:1], iota((z.req, 1), 0)], axis=0)
    attended = []
    for i in range(n):
        core = lax.rem(me + i, n)
        stacked = collect(z, back_ref, n, core).astype(BF16)
        attended.append(merged(z, stacked, owner, owns[i][:, : z.width], owns[i][:, z.width :]))
    mixed = dot(attended[0], out_ref[...])
    for i in range(1, n):
        next(copies).wait()
        mixed = mixed + dot(attended[i], out_refs[i - 1][...])
    mixed = (tokens_ref[...].astype(F32) + mixed).astype(BF16).astype(F32)
    mixed_ref[...] = mixed
    here_ref[...] = core_columns(mixed_ref, 0, n)[...]
    hidden_in = normalize(mixed, gain_ref[...]).astype(BF16)
    gate = upper = 0
    for at in deep:
        next(copies).wait()
        gate = gate + dot(hidden_in[:, at], gate_ref[at, :])
    gate = jax.nn.silu(gate)
    for at in deep:
        next(copies).wait()
        upper = upper + dot(hidden_in[:, at], up_ref[at, :])
    hidden = (gate * upper).astype(BF16)
    hidden_ref[...] = hidden
    for away_ref, down_ref in zip(away_refs, down_refs):
        total = 0
        for at in unit:
            next(copies).wait()
            total = total + dot(hidden[:, at], down_ref[at, :])
        away_ref[...] = total.astype(BF16)


def finish_kernel(hidden_ref, mixed_ref, down_ref, here_ref):
    here_ref[...] = mixed_ref[...] + dot(hidden_ref[...], down_ref[...])


VMEM = pl.BlockSpec(memory_space=pltpu.VMEM)
HBM = pl.BlockSpec(memory_space=pltpu.HBM)


def in_hbm(*arrays):
    return tuple(pltpu.with_memory_space_constraint(x, pltpu.HBM) for x in arrays)


def call(kernel, out, operands, specs, scratch=(), name=None, limit=16):
    return pl.pallas_call(
        kernel,
        out_shape=out,
        in_specs=specs,
        out_specs=[VMEM] * len(out),
        scratch_shapes=list(scratch),
        compiler_params=pltpu.CompilerParams(vmem_limit_bytes=int(limit * 1024 * 1024)),
        cost_estimate=pl.CostEstimate(flops=10**10, bytes_accessed=10**7, transcendentals=0),
        name=name,
    )(*operands)


def from_core(x, shift):
    n = lax.axis_size("head")
    return lax.ppermute(x, "head", [((i + shift) % n, i) for i in range(n)])


def all_cores(x):
    return [x] + [from_core(x, i) for i in range(1, lax.axis_size("head"))]


def body(
    tokens,
    norm_gain,
    w_query,
    w_key,
    w_value,
    w_out,
    ffn_gain,
    w_gate,
    w_up,
    w_down,
    keys,
    values,
    key_variate,
    query_variate,
    bias,
    lengths,
    order,
    live_blocks,
):
    groups = lax.axis_size("blk")
    head_count = lax.axis_size("head")
    z = Sizes(
        groups,
        head_count,
        tokens.shape[0],
        keys.shape[0],
        keys.shape[0] // live_blocks.shape[0],
        bias.shape[1],
        w_query.shape[1] // bias.shape[1],
    )
    d_model = tokens.shape[1]
    width_local = d_model // head_count
    row = lambda x: x.reshape(1, -1)
    operands = (row(lengths), row(order), tokens, row(norm_gain), w_query)
    ask, rows, places, home = call(
        functools.partial(ask_kernel, z),
        [
            jax.ShapeDtypeStruct((groups, z.slot, z.width), BF16),
            pltpu.VMEM((z.req, z.width + d_model), BF16),
            pltpu.VMEM((8, z.total), F32),
            pltpu.VMEM((z.slots, LANES), I32),
        ],
        in_hbm(*operands),
        [HBM] * len(operands),
        scratch=[pltpu.VMEM(x.shape, x.dtype) for x in operands]
        + [pltpu.SemaphoreType.DMA((len(operands) + 1,))],
        name="ask",
    )
    asked = lax.all_to_all(ask, "blk", 0, 0)
    early, small = (keys, values), (row(query_variate), row(live_blocks), row(key_variate), bias, w_key, w_value)
    keys_near, values_near, facts, own = call(
        functools.partial(first_load_kernel, z, len(early)),
        [pltpu.VMEM(x.shape, x.dtype) for x in early]
        + [pltpu.VMEM((8 + 2 * z.slots, z.pool), F32), pltpu.VMEM((z.req, z.width + LANES), BF16)],
        (places, rows) + in_hbm(*early, *small),
        [VMEM] * 2 + [HBM] * (len(early) + len(small)),
        scratch=[pltpu.VMEM(x.shape, x.dtype) for x in small]
        + [pltpu.SemaphoreType.DMA((len(early) + len(small),))],
        name="first_load",
    )
    w_out_after, _ = lax.optimization_barrier((w_out, own))
    outs = [w_out] + [from_core(w_out_after, i) for i in range(1, head_count)]
    owns = all_cores(own)
    back, done = call(
        functools.partial(attend_kernel, z),
        [jax.ShapeDtypeStruct((groups * head_count, z.slot, z.width + LANES), BF16), pltpu.VMEM((8, LANES), F32)],
        (asked, keys_near, values_near, facts),
        [VMEM] * 4,
        name="attend",
    )
    returned = lax.all_to_all(back, ("blk", "head"), 0, 0)
    late = (tokens, row(ffn_gain), w_out)
    units = w_down.shape[0]
    tokens_near, gain_near, out_near, down_near = call(
        functools.partial(second_load_kernel, z, len(late)),
        [pltpu.VMEM(x.shape, x.dtype) for x in late] + [pltpu.VMEM((units, width_local), BF16)],
        (done,) + in_hbm(*late, w_down),
        [VMEM] + [HBM] * (len(late) + 1),
        scratch=[pltpu.SemaphoreType.DMA((len(late) + 1,))],
        name="second_load",
    )
    given = (returned, home, tokens_near, gain_near, *owns, out_near)
    streamed = (*outs[1:], w_gate, w_up)
    hidden, here, *away = call(
        functools.partial(tail_kernel, z),
        [pltpu.VMEM((z.req, units), BF16), pltpu.VMEM((z.req, width_local), F32)]
        + [pltpu.VMEM((z.req, width_local), BF16)] * (head_count - 1),
        given + in_hbm(*streamed, w_down),
        [VMEM] * len(given) + [HBM] * (len(streamed) + 1),
        scratch=[pltpu.VMEM(x.shape, x.dtype) for x in streamed]
        + [pltpu.VMEM((units, width_local), BF16)] * (head_count - 1)
        + [
            pltpu.VMEM((z.req, d_model), F32),
            pltpu.SemaphoreType.DMA((head_count - 1 + 2 * STEPS + DOWN_STEPS * (head_count - 1),)),
        ],
        name="tail",
        limit=24,
    )
    arrived = [from_core(x, head_count - i) for i, x in enumerate(away, 1)]
    (here,) = call(
        finish_kernel,
        [pltpu.VMEM((z.req, width_local), F32)],
        (hidden, here, down_near),
        [VMEM] * 3,
        name="finish",
    )
    for x in arrived:
        here = here + x.astype(F32)
    return here.astype(BF16)


def solution(mesh):
    placed = (
        P("blk", None),
        P(),
        P(None, "head"),
        P(None, "head"),
        P(None, "head"),
        P("head", None),
        P(),
        P(None, "head"),
        P(None, "head"),
        P("head", None),
        P("blk", "head"),
        P("blk", "head"),
        P("blk"),
        P(),
        P(None, "head"),
        P(),
        P(),
        P("blk"),
    )
    return jax.shard_map(
        body, mesh=mesh, in_specs=placed, out_specs=P("blk", "head"), check_vma=False
    )
```

```python
import functools

import jax
import jax.numpy as jnp
from jax import lax
from jax.experimental import pallas as pl
from jax.experimental.pallas import tpu as pltpu
from jax.sharding import PartitionSpec as P

LANES = 128
SHORTEST = 17
FLOOR = -1e30
STEPS = 4
DOWN_STEPS = 4
F32 = jnp.float32
BF16 = jnp.bfloat16
I32 = jnp.int32


def cdiv(a, b):
    return -(-a // b)


def split_by(x, n):
    if n & (n - 1) == 0:
        return lax.shift_right_logical(x, n.bit_length() - 1), x & (n - 1)
    q = lax.div(x, n)
    return q, x - q * n


def iota(shape, dim):
    return lax.broadcasted_iota(I32, shape, dim)


def dot(a, b):
    return jnp.dot(a, b, preferred_element_type=F32)


def dot_exact(a, b):
    return jnp.dot(a, b, preferred_element_type=F32, precision=lax.Precision.HIGHEST)


def one_hot(mask):
    return jnp.where(mask, F32(1), F32(0)).astype(BF16)


def normalize(inputs, gain):
    mean_square = jnp.mean(inputs * inputs, axis=-1, keepdims=True)
    return inputs * lax.rsqrt(mean_square + 1e-05) * gain


class Sizes:
    def __init__(self, groups, cores, req_dev, pool_dev, block, heads, head_dim):
        self.groups, self.cores, self.req, self.pool = groups, cores, req_dev, pool_dev
        self.block, self.heads, self.dim = block, heads, head_dim
        self.total = groups * req_dev
        most = (pool_dev - 2) // SHORTEST + 2
        self.slot = cdiv(most, groups)
        self.slots = groups * self.slot
        self.width = heads * head_dim
        self.chunks = self.width // LANES
        self.wide = min(self.width, 2 * LANES)
        self.pair = LANES // head_dim


def deal(z, rows, out_ref, cores=1):
    for g in range(z.groups):
        part = rows[g * z.slot : (g + 1) * z.slot].astype(BF16)
        for core in range(cores):
            out_ref[g * cores + core] = part


def collect(z, ref, cores=1, core=0):
    return jnp.concatenate([ref[g * cores + core].astype(F32) for g in range(z.groups)], axis=0)


def place_rows(lengths, order, variate, step=512):
    total = order.shape[1]
    step = min(step, total)
    sub = iota((16, total), 0)
    table = jnp.where(
        sub == 0,
        lax.shift_right_logical(lengths, 6),
        jnp.where(sub == 1, lengths & 63, jnp.where(sub == 2, variate, 0)),
    )
    table = table.astype(F32).astype(BF16)
    request = iota((total, step), 0)
    found, sums = [], []
    for at in range(0, total, step):
        found.append(dot(table, one_hot(request == order[:, at : at + step])))
    ordered = jnp.concatenate(found, axis=1) if len(found) > 1 else found[0]
    ordered_low = ordered.astype(BF16)
    for at in range(0, total, step):
        before = one_hot(iota((at + step, step), 0) <= iota((at + step, step), 1) + at)
        sums.append(dot(ordered_low[:, : at + step], before))
    summed = jnp.concatenate(sums, axis=1) if len(sums) > 1 else sums[0]
    ends = summed[0:1] * 64.0 + summed[1:2]
    starts = ends - (ordered[0:1] * 64.0 + ordered[1:2])
    return starts, ends, ordered[2:3]


def fetch(pairs, sems):
    copies = [pltpu.make_async_copy(src, dst, sems.at[i]) for i, (src, dst) in enumerate(pairs)]
    for copy in copies:
        copy.start()
    return copies


def choose(z, starts, ends, home_of, turn, home, pool):
    low = (pool * z.pool).astype(F32)
    first = jnp.sum(jnp.where(ends <= low, F32(1), F32(0)), axis=1, keepdims=True)
    first = first + (turn * z.groups).astype(F32)
    place = iota((z.slots, z.total), 1).astype(F32)
    return (
        (home_of == home)
        & (starts < low + F32(z.pool))
        & (place >= first)
        & (place < first + F32(z.groups))
    )


def ask_kernel(z, lengths_hbm, order_hbm, variate_hbm, tokens_hbm, gain_hbm, w_query_hbm, ask_ref, rows_ref,
               places_ref, home_ref, lengths_ref, order_ref, variate_ref, tokens_ref, gain_ref, w_query_ref,
               sems):
    me = lax.axis_index("blk")
    half = w_query_hbm.shape[0] // 2
    copies = fetch(
        [
            (lengths_hbm, lengths_ref),
            (order_hbm, order_ref),
            (variate_hbm, variate_ref),
            (tokens_hbm, tokens_ref),
            (gain_hbm, gain_ref),
            (w_query_hbm.at[:half, :], w_query_ref.at[:half, :]),
            (w_query_hbm.at[half:, :], w_query_ref.at[half:, :]),
        ],
        sems,
    )
    for copy in copies[:3]:
        copy.wait()
    order = order_ref[...]
    starts, ends, variates = place_rows(lengths_ref[...], order, variate_ref[...])
    home_of, local = split_by(order, z.req)
    places_ref[0:1, :] = starts
    places_ref[1:2, :] = ends
    places_ref[2:3, :] = variates
    places_ref[3:4, :] = home_of.astype(F32)
    other, turn = split_by(iota((z.slots, 1), 0), z.slot)
    mine = choose(z, starts, ends, home_of, turn, me, other)
    row = jnp.sum(jnp.where(mine, local.astype(F32) + 1.0, F32(0)), axis=1, keepdims=True) - 1.0
    row = row.astype(I32)
    home_ref[...] = jnp.broadcast_to(row, home_ref.shape)

    for copy in copies[3:]:
        copy.wait()
    normed = normalize(tokens_ref[...].astype(F32), gain_ref[...]).astype(BF16)
    rows_ref[:, z.width :] = normed
    query = dot(normed, w_query_ref[...]).astype(BF16)
    rows_ref[:, : z.width] = query
    deal(z, dot(one_hot(row == iota((z.slots, z.req), 1)), query), ask_ref)


def slot_facts(z, places_ref, live, key_variate, bias, facts_ref):
    me = lax.axis_index("blk")
    starts, ends, variates = places_ref[0:1, :], places_ref[1:2, :], places_ref[2:3, :]
    home_of = places_ref[3:4, :].astype(I32)
    other, turn = split_by(iota((z.slots, 1), 0), z.slot)
    theirs = choose(z, starts, ends, home_of, turn, other, jnp.full((1, 1), me, I32))
    low = (me * z.pool).astype(F32)
    begin = jnp.sum(jnp.where(theirs, starts - low, F32(0)), axis=1, keepdims=True)
    finish = jnp.sum(jnp.where(theirs, ends - low, F32(0)), axis=1, keepdims=True)
    kind = jnp.sum(jnp.where(theirs, variates, F32(0)), axis=1, keepdims=True)
    blocks = live.shape[1]
    spread = one_hot(
        split_by(iota((blocks, z.pool), 1), z.block)[0] == iota((blocks, z.pool), 0)
    )
    live = jnp.broadcast_to(live.astype(F32).astype(BF16), (16, blocks))
    kinds = jnp.where(dot(live, spread)[:1] > 0, key_variate, -1)
    kinds = kinds.astype(F32)
    token = iota((z.slots, z.pool), 1).astype(F32)
    used = (token >= begin) & (token < finish) & (kinds >= 0)
    facts_ref[: z.slots, :] = jnp.where(kinds == kind, F32(1), F32(0))
    facts_ref[z.slots : 2 * z.slots, :] = jnp.where(used, F32(0), F32(FLOOR))
    facts_ref[2 * z.slots : 2 * z.slots + 2, 0 : z.heads] = bias


def pieces(z, columns):
    rows = columns[0].shape[0]
    lane = iota((rows, LANES), 1)
    full = jnp.zeros((rows, LANES), F32)
    for h, column in enumerate(columns):
        full = jnp.where((lane & (z.heads - 1)) == h, column, full)
    high = full.astype(BF16).astype(F32)
    rest = full - high
    middle = rest.astype(BF16).astype(F32)
    last = rest - middle
    n = z.heads
    return jnp.where(
        lane < n, high, jnp.where(lane < 2 * n, middle, jnp.where(lane < 3 * n, last, F32(0)))
    )


def first_load_kernel(z, count, places_ref, rows_ref, *refs):
    far, small = refs[:count], refs[count : count + 5]
    near, (facts_ref, own_ref) = refs[count + 5 : 2 * count + 5], refs[2 * count + 5 : 2 * count + 7]
    held, sems = refs[2 * count + 7 : -1], refs[-1]
    copies = fetch([*zip(small, held), *zip(far, near)], sems)
    live_ref, key_variate_ref, bias_ref, w_key_ref, w_value_ref = held
    for copy in copies[:3]:
        copy.wait()
    slot_facts(z, places_ref, live_ref[...], key_variate_ref[...], bias_ref[...], facts_ref)
    normed = rows_ref[:, z.width :]
    copies[3].wait()
    key_new = dot(normed, w_key_ref[...]).astype(BF16)
    product = rows_ref[:, : z.width].astype(F32) * key_new.astype(F32)
    columns = []
    for h in range(z.heads):
        c, inner = divmod(h, z.pair)
        part = product[:, c * LANES : (c + 1) * LANES]
        lane_head = split_by(iota(part.shape, 1), z.dim)[0]
        raw = jnp.sum(jnp.where(lane_head == inner, part, F32(0)), axis=1, keepdims=True)
        columns.append(raw * F32(z.dim**-0.5) + bias_ref[0:1, h : h + 1])
    own_ref[:, z.width :] = pieces(z, columns).astype(BF16)
    copies[4].wait()
    own_ref[:, : z.width] = dot(normed, w_value_ref[...]).astype(BF16)
    for copy in copies[5:]:
        copy.wait()


def core_columns(ref, shift, cores):
    width = ref.shape[-1] // cores
    core = lax.rem(lax.axis_index("head") + shift, cores)
    return ref.at[:, pl.ds(pl.multiple_of(core * width, width), width)]


def second_load_kernel(z, count, after_ref, *refs):
    del after_ref
    pairs = list(zip(refs[:count], refs[count + 1 : 2 * count + 1]))
    pairs.append((core_columns(refs[count], 0, z.cores), refs[-2]))
    for copy in fetch(pairs, refs[-1]):
        copy.wait()


def attend_kernel(z, ask_ref, keys_ref, values_ref, facts_ref, back_ref, done_ref):
    done_ref[...] = jnp.zeros(done_ref.shape, F32)
    stacked = collect(z, ask_ref)
    same, unused = facts_ref[: z.slots, :], facts_ref[z.slots : 2 * z.slots, :]
    bias = facts_ref[2 * z.slots : 2 * z.slots + 2, 0 : z.heads]
    lane = split_by(iota((z.slots, z.wide), 1), z.dim)[0]
    many = z.wide // z.dim
    columns, parts = [], []
    for c in range(z.width // z.wide):
        chunk = slice(c * z.wide, (c + 1) * z.wide)
        asked = stacked[:, chunk]
        asked = (asked * F32(z.dim**-0.5)).astype(BF16)
        blocks = jnp.concatenate(
            [jnp.where(lane == i, asked, jnp.zeros_like(asked)) for i in range(many)], axis=0
        )
        score = lax.dot_general(
            blocks, keys_ref[:, chunk], (((1,), (1,)), ((), ())), preferred_element_type=F32
        )
        weights, scale = [], []
        for i in range(many):
            h = c * many + i
            one = score[i * z.slots : (i + 1) * z.slots]
            one = one + (same * (bias[0:1, h : h + 1] - bias[1:2, h : h + 1]) + unused)
            top = jnp.maximum(jnp.max(one, axis=1, keepdims=True), F32(FLOOR * 0.1))
            weight = jnp.exp(one - top)
            total = jnp.sum(weight, axis=1, keepdims=True)
            some = total > 0
            safe = jnp.where(some, total, F32(1))
            columns.append(jnp.where(some, top + bias[1:2, h : h + 1] + jnp.log(safe), F32(FLOOR)))
            scale.append(1.0 / safe)
            weights.append(weight.astype(BF16))
        summed = dot(jnp.concatenate(weights, axis=0), values_ref[:, chunk])
        part = summed[: z.slots] * scale[0]
        for i in range(1, many):
            part = jnp.where(lane == i, summed[i * z.slots : (i + 1) * z.slots] * scale[i], part)
        parts.append(part)
    parts.append(pieces(z, columns))
    deal(z, jnp.concatenate(parts, axis=1), back_ref, z.cores)


def merged(z, stacked, owner, value, stat):
    stat = jnp.concatenate([stacked[:, z.width :], stat], axis=0)
    rows = z.slots + z.req
    wide = z.heads * z.req
    head_at, _ = split_by(iota((LANES, wide), 1), z.req)
    from_lane = iota((LANES, wide), 0)
    spread = one_hot(((from_lane & (z.heads - 1)) == head_at) & (from_lane < 3 * z.heads))
    level = dot(stat, spread)
    _, request = split_by(iota((rows, wide), 1), z.req)
    match = owner == request
    level = jnp.where(match, level, F32(FLOOR))
    top = jnp.max(level, axis=0, keepdims=True)
    weight = jnp.where(match, jnp.exp(level - top), F32(0))
    weight = weight * (1.0 / jnp.sum(weight, axis=0, keepdims=True))
    high = weight.astype(BF16)
    held = jnp.concatenate([stacked[:, : z.width], value], axis=0)
    dims = (((0,), (0,)), ((), ()))
    summed = lax.dot_general(high, held, dims, preferred_element_type=F32)
    lane = split_by(iota((z.req, z.width), 1), z.dim)[0]
    attended = summed[: z.req]
    for h in range(1, z.heads):
        attended = jnp.where(lane == h, summed[h * z.req : (h + 1) * z.req], attended)
    return attended.astype(BF16)


def tail_kernel(z, *refs):
    n = z.cores
    back_ref, home_ref, tokens_ref, gain_ref = refs[:4]
    owns, out_ref, refs = refs[4 : 4 + n], refs[4 + n], refs[5 + n :]
    out_hbms, (gate_hbm, up_hbm, down_hbm), refs = refs[: n - 1], refs[n - 1 : n + 2], refs[n + 2 :]
    hidden_ref, here_ref, away_refs, refs = refs[0], refs[1], refs[2 : n + 1], refs[n + 1 :]
    out_refs, (gate_ref, up_ref), refs = refs[: n - 1], refs[n - 1 : n + 1], refs[n + 1 :]
    down_refs, mixed_ref, sems = refs[: n - 1], refs[n - 1], refs[n]

    def cut(rows, count):
        return [slice(i * (rows // count), (i + 1) * (rows // count)) for i in range(count)]

    deep, unit = cut(gate_ref.shape[0], STEPS), cut(down_hbm.shape[0], DOWN_STEPS)
    pairs = list(zip(out_hbms, out_refs))
    pairs += [(gate_hbm.at[at, :], gate_ref.at[at, :]) for at in deep]
    pairs += [(up_hbm.at[at, :], up_ref.at[at, :]) for at in deep]
    for i in range(1, n):
        columns = core_columns(down_hbm, i, n)
        pairs += [(columns.at[at, :], down_refs[i - 1].at[at, :]) for at in unit]
    copies = iter(fetch(pairs, sems))
    me = lax.axis_index("head")
    owner = jnp.concatenate([home_ref[:, 0:1], iota((z.req, 1), 0)], axis=0)
    attended = []
    for i in range(n):
        core = lax.rem(me + i, n)
        stacked = collect(z, back_ref, n, core).astype(BF16)
        attended.append(merged(z, stacked, owner, owns[i][:, : z.width], owns[i][:, z.width :]))
    mixed = dot(attended[0], out_ref[...])
    for i in range(1, n):
        next(copies).wait()
        mixed = mixed + dot(attended[i], out_refs[i - 1][...])
    mixed = (tokens_ref[...].astype(F32) + mixed).astype(BF16).astype(F32)
    mixed_ref[...] = mixed
    here_ref[...] = core_columns(mixed_ref, 0, n)[...]
    hidden_in = normalize(mixed, gain_ref[...]).astype(BF16)
    gate = upper = 0
    for at in deep:
        next(copies).wait()
        gate = gate + dot(hidden_in[:, at], gate_ref[at, :])
    gate = jax.nn.silu(gate)
    for at in deep:
        next(copies).wait()
        upper = upper + dot(hidden_in[:, at], up_ref[at, :])
    hidden = (gate * upper).astype(BF16)
    hidden_ref[...] = hidden
    for away_ref, down_ref in zip(away_refs, down_refs):
        total = 0
        for at in unit:
            next(copies).wait()
            total = total + dot(hidden[:, at], down_ref[at, :])
        away_ref[...] = total.astype(BF16)


def finish_kernel(hidden_ref, mixed_ref, down_ref, here_ref):
    here_ref[...] = mixed_ref[...] + dot(hidden_ref[...], down_ref[...])


VMEM = pl.BlockSpec(memory_space=pltpu.VMEM)
HBM = pl.BlockSpec(memory_space=pltpu.HBM)


def in_hbm(*arrays):
    return tuple(pltpu.with_memory_space_constraint(x, pltpu.HBM) for x in arrays)


def call(kernel, out, operands, specs, scratch=(), name=None, limit=16):
    return pl.pallas_call(
        kernel,
        out_shape=out,
        in_specs=specs,
        out_specs=[VMEM] * len(out),
        scratch_shapes=list(scratch),
        compiler_params=pltpu.CompilerParams(vmem_limit_bytes=int(limit * 1024 * 1024)),
        cost_estimate=pl.CostEstimate(flops=10**10, bytes_accessed=10**7, transcendentals=0),
        name=name,
    )(*operands)


def from_core(x, shift):
    n = lax.axis_size("head")
    return lax.ppermute(x, "head", [((i + shift) % n, i) for i in range(n)])


def all_cores(x):
    return [x] + [from_core(x, i) for i in range(1, lax.axis_size("head"))]


def body(
    tokens,
    norm_gain,
    w_query,
    w_key,
    w_value,
    w_out,
    ffn_gain,
    w_gate,
    w_up,
    w_down,
    keys,
    values,
    key_variate,
    query_variate,
    bias,
    lengths,
    order,
    live_blocks,
):
    groups = lax.axis_size("blk")
    head_count = lax.axis_size("head")
    z = Sizes(
        groups,
        head_count,
        tokens.shape[0],
        keys.shape[0],
        keys.shape[0] // live_blocks.shape[0],
        bias.shape[1],
        w_query.shape[1] // bias.shape[1],
    )
    d_model = tokens.shape[1]
    width_local = d_model // head_count
    row = lambda x: x.reshape(1, -1)
    operands = (row(lengths), row(order), row(query_variate), tokens, row(norm_gain), w_query)
    ask, rows, places, home = call(
        functools.partial(ask_kernel, z),
        [
            jax.ShapeDtypeStruct((groups, z.slot, z.width), BF16),
            pltpu.VMEM((z.req, z.width + d_model), BF16),
            pltpu.VMEM((8, z.total), F32),
            pltpu.VMEM((z.slots, LANES), I32),
        ],
        in_hbm(*operands),
        [HBM] * len(operands),
        scratch=[pltpu.VMEM(x.shape, x.dtype) for x in operands]
        + [pltpu.SemaphoreType.DMA((len(operands) + 1,))],
        name="ask",
    )
    asked = lax.all_to_all(ask, "blk", 0, 0)
    early, small = (keys, values), (row(live_blocks), row(key_variate), bias, w_key, w_value)
    keys_near, values_near, facts, own = call(
        functools.partial(first_load_kernel, z, len(early)),
        [pltpu.VMEM(x.shape, x.dtype) for x in early]
        + [pltpu.VMEM((8 + 2 * z.slots, z.pool), F32), pltpu.VMEM((z.req, z.width + LANES), BF16)],
        (places, rows) + in_hbm(*early, *small),
        [VMEM] * 2 + [HBM] * (len(early) + len(small)),
        scratch=[pltpu.VMEM(x.shape, x.dtype) for x in small]
        + [pltpu.SemaphoreType.DMA((len(early) + len(small),))],
        name="first_load",
    )
    w_out_after, _ = lax.optimization_barrier((w_out, own))
    outs = [w_out] + [from_core(w_out_after, i) for i in range(1, head_count)]
    owns = all_cores(own)
    back, done = call(
        functools.partial(attend_kernel, z),
        [jax.ShapeDtypeStruct((groups * head_count, z.slot, z.width + LANES), BF16), pltpu.VMEM((8, LANES), F32)],
        (asked, keys_near, values_near, facts),
        [VMEM] * 4,
        name="attend",
    )
    returned = lax.all_to_all(back, ("blk", "head"), 0, 0)
    late = (tokens, row(ffn_gain), w_out)
    units = w_down.shape[0]
    tokens_near, gain_near, out_near, down_near = call(
        functools.partial(second_load_kernel, z, len(late)),
        [pltpu.VMEM(x.shape, x.dtype) for x in late] + [pltpu.VMEM((units, width_local), BF16)],
        (done,) + in_hbm(*late, w_down),
        [VMEM] + [HBM] * (len(late) + 1),
        scratch=[pltpu.SemaphoreType.DMA((len(late) + 1,))],
        name="second_load",
    )
    given = (returned, home, tokens_near, gain_near, *owns, out_near)
    streamed = (*outs[1:], w_gate, w_up)
    hidden, here, *away = call(
        functools.partial(tail_kernel, z),
        [pltpu.VMEM((z.req, units), BF16), pltpu.VMEM((z.req, width_local), F32)]
        + [pltpu.VMEM((z.req, width_local), BF16)] * (head_count - 1),
        given + in_hbm(*streamed, w_down),
        [VMEM] * len(given) + [HBM] * (len(streamed) + 1),
        scratch=[pltpu.VMEM(x.shape, x.dtype) for x in streamed]
        + [pltpu.VMEM((units, width_local), BF16)] * (head_count - 1)
        + [
            pltpu.VMEM((z.req, d_model), F32),
            pltpu.SemaphoreType.DMA((head_count - 1 + 2 * STEPS + DOWN_STEPS * (head_count - 1),)),
        ],
        name="tail",
        limit=24,
    )
    arrived = [from_core(x, head_count - i) for i, x in enumerate(away, 1)]
    (here,) = call(
        finish_kernel,
        [pltpu.VMEM((z.req, width_local), F32)],
        (hidden, here, down_near),
        [VMEM] * 3,
        name="finish",
    )
    for x in arrived:
        here = here + x.astype(F32)
    return here.astype(BF16)


def solution(mesh):
    placed = (
        P("blk", None),
        P(),
        P(None, "head"),
        P(None, "head"),
        P(None, "head"),
        P("head", None),
        P(),
        P(None, "head"),
        P(None, "head"),
        P("head", None),
        P("blk", "head"),
        P("blk", "head"),
        P("blk"),
        P(),
        P(None, "head"),
        P(),
        P(),
        P("blk"),
    )
    return jax.shard_map(
        body, mesh=mesh, in_specs=placed, out_specs=P("blk", "head"), check_vma=False
    )
```
